256 devices in a mesh: ctx: 64 (over z, y, core), head: 4 (over x).
Axes of the slice: x: 4, y: 4, z: 8, core: 2. Of those that a mesh axis runs over, the one named last changes fastest.
Arguments:
- queries: bfloat16 [8192, 8192], P('ctx', 'head'), may hold values from -6 to 6
- key_states: bfloat16 [8192, 1024], P('ctx', 'head'), may hold values from -6 to 6
- value_states: bfloat16 [8192, 1024], P('ctx', 'head'), may hold values from -6 to 6
- keep_pages: int32 [8, 64, 8], P('head', 'ctx'), may hold values from 0 to 7, each once within a row
- keep_count: int32 [8, 64], P('head'), may hold values from 1 to 8, as said below
- dest_slot: int32 [8, 64, 8], P('head'), may hold values from 0 to 511, as said below
Outputs:
- attention: bfloat16 [8192, 8192], P('ctx', 'head')
- key_importance: float32 [8192], P('ctx')
- page_tiles: bfloat16 [64, 8, 8, 4096], P('ctx', 'head')
- page_scale: float32 [64, 8, 8, 2], P('ctx', 'head')
- key_bounds: float32 [64, 8, 8, 2, 128], P('ctx', 'head')
- page_score: float32 [64, 8, 8], P('ctx', 'head')
The draws below stay inside these ranges and needn't reach their ends.
Inputs may be any that keep to these rules, and one draw needn't show every extreme that they name: `keep_pages`: every list holds each page number of its block once. `keep_count`: some block of each KV head keeps all of its 8 pages. `dest_slot`: within one KV head, the entries of all blocks name distinct slots, so each owner has 8 places for each KV head. The owner of an entry of block c is (c + d) mod 64 with 0 <= d < 8; for each KV head and block, every such d is named by the same number of entries of the list, 1 of them.
All inputs are finite; a program needn't handle non-finite values. Where the reference program divides by a largest or mean magnitude, that divisor is 1e-20 or more.
Results may differ from the reference program's by a relative error of at most 0.0055.
Values may be sent and summed in bfloat16 or wider, within the bound.
A program may use at most 64 MiB of HBM per device.

```python
import math
import jax
import jax.numpy as jnp
from jax import lax

HEAD_DIM = 128
QUERY_HEAD_COUNT = 64
KV_HEADS = 8
PAGE = 16
HEADS_PER_GROUP = 8
SEQ_LEN = 8192
P_DEV = 8
SPAN = 8
N_CTX = 64


def draw_queries(key, part):
    key = jax.random.fold_in(key, 5)
    value_rows = jax.random.truncated_normal(key, -6.0, 6.0, (SEQ_LEN, QUERY_HEAD_COUNT * HEAD_DIM), jnp.float32)
    return value_rows.astype(jnp.bfloat16)


def draw_key_states(key, part):
    key = jax.random.fold_in(key, 9)
    value_rows = jax.random.truncated_normal(key, -6.0, 6.0, (SEQ_LEN, KV_HEADS * HEAD_DIM), jnp.float32)
    return value_rows.astype(jnp.bfloat16)


def draw_keep_count(key, part):
    key = jax.random.fold_in(key, 21)
    first_key, second_key, third_key = jax.random.split(key, 3)
    first = jax.random.randint(first_key, (KV_HEADS, N_CTX), 1, P_DEV + 1)
    second = jax.random.randint(second_key, (KV_HEADS, N_CTX), 1, P_DEV + 1)
    counts = jnp.maximum(first, second)
    chosen = jax.random.randint(third_key, (KV_HEADS,), 0, N_CTX)
    counts = counts.at[jnp.arange(KV_HEADS), chosen].set(P_DEV)
    return counts.astype(jnp.int32)


def draw_dest_slot(key, part):
    key = jax.random.fold_in(key, 33)
    perm_key, place_key = jax.random.split(key, 2)
    per_owner = P_DEV // SPAN
    orders = jax.vmap(lambda k: jax.random.permutation(k, P_DEV))(jax.random.split(perm_key, KV_HEADS * N_CTX))
    orders = orders.reshape(KV_HEADS, N_CTX, P_DEV).astype(jnp.int32)
    offsets = orders // per_owner
    owner = (jnp.arange(N_CTX, dtype=jnp.int32)[None, :, None] + offsets) % N_CTX
    rotate = jax.random.randint(place_key, (KV_HEADS, N_CTX), 0, P_DEV)
    head_ids = jnp.arange(KV_HEADS)[:, None, None]
    place = (orders + rotate[head_ids, owner]) % P_DEV
    return (owner * P_DEV + place).astype(jnp.int32)


def levels(key, extent, cuts, low, largest):
    factor_of, own = 1.0, jax.random.fold_in(key, 6)
    for position, blocks in cuts:
        heights = jnp.exp(jax.random.uniform(jax.random.fold_in(own, position), (blocks,), jnp.float32, low / len(cuts), largest / len(cuts)))
        factor_of = factor_of * jnp.repeat(heights, extent[position] // blocks).reshape([-1 if axis == position else 1 for axis in range(len(extent))])
    return factor_of


def normal_values(key, extent, deviation, limit, shards=(), held_as=jnp.bfloat16):
    drawn = deviation * jax.random.normal(key, extent, jnp.float32)
    if shards:
        drawn = drawn * levels(key, extent, shards, -0.22, 0.18)
    return jnp.clip(drawn, -limit, limit).astype(held_as)


def setup_inputs(seed: int = 0) -> dict:
    arg_keys = jax.random.split(jax.random.key(seed), 7)
    return {
        "queries": draw_queries(jax.random.fold_in(arg_keys[6], 71), 0),
        "key_states": draw_key_states(jax.random.fold_in(arg_keys[6], 71), 0),
        "value_states": normal_values(arg_keys[2], (SEQ_LEN, KV_HEADS * HEAD_DIM), 1.0, 6.0, ((0, 64), (1, 4))),
        "keep_pages": jax.vmap(lambda own: jax.random.permutation(own, P_DEV))(jax.random.split(arg_keys[3], KV_HEADS * N_CTX)).reshape((KV_HEADS, N_CTX, P_DEV)).astype(jnp.int32),
        "keep_count": draw_keep_count(jax.random.fold_in(arg_keys[6], 71), 0),
        "dest_slot": draw_dest_slot(jax.random.fold_in(arg_keys[6], 71), 0),
    }


negative_fill = -1e+30
quant_levels = 7.0
amax_epsilon = 1e-06

def requantize(flat_tiles):
    entries = flat_tiles.shape[0]
    halves = flat_tiles.reshape(entries, 2, PAGE * HEAD_DIM).astype(jnp.float32)
    amax = lax.optimization_barrier(jnp.max(jnp.abs(halves), axis=2))
    normalized = (halves * quant_levels / (amax + amax_epsilon)[..., None]).astype(jnp.bfloat16)
    key_rows = halves[:, 0].reshape(entries, PAGE, HEAD_DIM)
    bounds = jnp.stack([lax.optimization_barrier(jnp.min(key_rows, axis=1)), lax.optimization_barrier(jnp.max(key_rows, axis=1))], axis=1)
    return (normalized.reshape(entries, 2 * PAGE * HEAD_DIM), amax / quant_levels, bounds)

def per_head_sweep(head_queries, head_keys, head_values):
    block_rows = math.gcd(SEQ_LEN, 512)
    block_count = SEQ_LEN // block_rows
    score_scale = 1.0 / math.sqrt(HEAD_DIM)
    key_pos = jnp.arange(SEQ_LEN, dtype=jnp.int32)
    query_blocks = head_queries.reshape(block_count, block_rows, HEADS_PER_GROUP, HEAD_DIM)

    def block_scores(block_index):
        query_pos = block_index * block_rows + jnp.arange(block_rows, dtype=jnp.int32)
        visible = key_pos[None, :] <= query_pos[:, None]
        scores = jnp.einsum('tgd,rd->gtr', query_blocks[block_index], head_keys, precision=lax.Precision.HIGHEST) * score_scale
        return (visible, jnp.where(visible, scores, negative_fill))

    def first_pass(block_index):
        visible, scores = block_scores(block_index)
        row_max = lax.optimization_barrier(jnp.max(scores, axis=-1))
        weights = jnp.where(visible, jnp.exp(scores - row_max[..., None]), 0.0)
        row_total = lax.optimization_barrier(jnp.sum(weights, axis=-1))
        rounded = lax.optimization_barrier(weights.astype(jnp.bfloat16)).astype(jnp.float32)
        mixed = jnp.einsum('gtr,rd->tgd', rounded, head_values, precision=lax.Precision.HIGHEST)
        mixed = mixed / jnp.transpose(row_total)[..., None]
        return (mixed.astype(jnp.bfloat16), row_max + jnp.log(row_total))
    attn_blocks, lse = lax.map(first_pass, jnp.arange(block_count, dtype=jnp.int32))

    def second_pass(column, block_index):
        visible, scores = block_scores(block_index)
        weights = jnp.where(visible, jnp.exp(scores - lse[block_index][..., None]), 0.0)
        return (column + lax.optimization_barrier(jnp.sum(weights, axis=(0, 1))), None)
    column, unused = lax.scan(second_pass, jnp.zeros((SEQ_LEN,), jnp.float32), jnp.arange(block_count, dtype=jnp.int32))
    return (attn_blocks.reshape(SEQ_LEN, HEADS_PER_GROUP, HEAD_DIM), column)

def reference(queries, key_states, value_states, keep_pages, keep_count, dest_slot):
    grouped = queries.reshape(SEQ_LEN, KV_HEADS, HEADS_PER_GROUP, HEAD_DIM)
    keys_by_head = key_states.reshape(SEQ_LEN, KV_HEADS, HEAD_DIM)
    values_by_head = value_states.reshape(SEQ_LEN, KV_HEADS, HEAD_DIM)

    def per_head(head_index):
        return per_head_sweep(lax.dynamic_index_in_dim(grouped, head_index, 1, keepdims=False).astype(jnp.float32), lax.dynamic_index_in_dim(keys_by_head, head_index, 1, keepdims=False).astype(jnp.float32), lax.dynamic_index_in_dim(values_by_head, head_index, 1, keepdims=False).astype(jnp.float32))
    attn_heads, columns = lax.map(per_head, jnp.arange(KV_HEADS, dtype=jnp.int32))
    attention = jnp.transpose(attn_heads, (1, 0, 2, 3)).reshape(SEQ_LEN, QUERY_HEAD_COUNT * HEAD_DIM)
    positions = jnp.arange(SEQ_LEN, dtype=jnp.int32)
    column_score = columns * (SEQ_LEN / HEADS_PER_GROUP) / (SEQ_LEN - positions).astype(jnp.float32)
    key_importance = lax.optimization_barrier(jnp.sum(column_score, axis=0))
    page_mean = column_score.reshape(KV_HEADS, N_CTX, P_DEV, PAGE).mean(axis=-1)
    tile_width = 2 * PAGE * HEAD_DIM
    key_pages = jnp.transpose(key_states.reshape(N_CTX, P_DEV, PAGE, KV_HEADS, HEAD_DIM), (3, 0, 1, 2, 4)).reshape(KV_HEADS, N_CTX, P_DEV, PAGE * HEAD_DIM)
    value_pages = jnp.transpose(value_states.reshape(N_CTX, P_DEV, PAGE, KV_HEADS, HEAD_DIM), (3, 0, 1, 2, 4)).reshape(KV_HEADS, N_CTX, P_DEV, PAGE * HEAD_DIM)
    tiles = jnp.concatenate([key_pages, value_pages], axis=-1)
    kept_tiles = jnp.take_along_axis(tiles, keep_pages[..., None], axis=2)
    kept_score = jnp.take_along_axis(page_mean, keep_pages, axis=2)
    normalized, scales, bounds = requantize(kept_tiles.reshape(-1, tile_width))
    owner = dest_slot // P_DEV
    place = dest_slot % P_DEV
    valid = jnp.arange(P_DEV, dtype=jnp.int32)[None, None, :] < keep_count[:, :, None]
    owner = jnp.where(valid, owner, N_CTX).astype(jnp.int32)
    head_ids = jnp.broadcast_to(jnp.arange(KV_HEADS, dtype=jnp.int32)[:, None, None], owner.shape)
    page_tiles = jnp.zeros((N_CTX, KV_HEADS, P_DEV, tile_width), jnp.bfloat16).at[owner, head_ids, place].set(normalized.reshape(KV_HEADS, N_CTX, P_DEV, tile_width), mode='drop')
    page_scale = jnp.zeros((N_CTX, KV_HEADS, P_DEV, 2), jnp.float32).at[owner, head_ids, place].set(scales.reshape(KV_HEADS, N_CTX, P_DEV, 2), mode='drop')
    key_bounds = jnp.zeros((N_CTX, KV_HEADS, P_DEV, 2, HEAD_DIM), jnp.float32).at[owner, head_ids, place].set(bounds.reshape(KV_HEADS, N_CTX, P_DEV, 2, HEAD_DIM), mode='drop')
    page_score = jnp.zeros((N_CTX, KV_HEADS, P_DEV), jnp.float32).at[owner, head_ids, place].set(kept_score, mode='drop')
    return (attention, key_importance, page_tiles, page_scale, key_bounds, page_score)
```

```python
import functools

import jax
import jax.numpy as jnp
from jax import lax
from jax.experimental import pallas as pl
from jax.experimental.pallas import tpu as pltpu
from jax.sharding import PartitionSpec as P

MESH = pl.DeviceIdType.MESH
F32 = jnp.float32
BF16 = jnp.bfloat16
NZ, NY, NC, NX = 8, 4, 2, 4
NCTX = NZ * NY * NC
BLK = 128
SLAB = NY * NC * BLK
ROWS = 2 * 8 * BLK
SPAN = 8
SCALE2 = 1.4426950408889634 / 128.0**0.5
LANES = SLAB // 128


def picks_kernel(pages_ref, count_ref, slot_ref, w_ref, r_ref):
    me = lax.axis_index("ctx")
    w_ref[...] = jnp.zeros_like(w_ref)
    r_ref[...] = jnp.zeros_like(r_ref)
    one = jnp.ones((1, 128), F32)

    def entry(e, carry):
        h = e // 8
        j = e % 8
        slot = slot_ref[h, me, j]
        off = lax.rem(slot // 8 - me + NCTX, NCTX)

        @pl.when(j < count_ref[h, me])
        def _():
            w_ref[pl.ds((off * 2 + h) * 8 + pages_ref[h, 0, j], 1), :] = one

        return carry

    lax.fori_loop(0, 16, entry, 0)

    def source(e, carry):
        d = e // 16
        h = (e // 8) % 2
        j = e % 8
        src = lax.rem(me - d + NCTX, NCTX)
        slot = slot_ref[h, src, j]

        @pl.when((j < count_ref[h, src]) & (slot // 8 == me))
        def _():
            r_ref[pl.ds((d * 2 + h) * 8 + lax.rem(slot, 8), 1), :] = one

        return carry

    lax.fori_loop(0, 128, source, 0)


def qk(a, b):
    return lax.dot_general(a, b, (((1,), (1,)), ((), ())), preferred_element_type=F32)


def main_kernel(
    q_ref, k_ref, v_ref, w_ref, r_ref,
    att_ref, imp_ref, tile_ref, scale_ref, bound_ref, score_ref,
    qb, kvb, prob, mx, run_m, run_l, acc, osend, csum, csr, tot8, t2, impb, impr, tsend, trecv,
    ssend, srecv, loc_sem, sib_s, sib_r, ya_s, ya_r, yb_s, yb_r, ra_s, ra_r, rb_s, rb_r,
    pg_s, pg_r, c1_s, c1_r, c2_s, c2_r, im_s, im_r, sc_s, sc_r, o_s, o_r,
):
    me = lax.axis_index("ctx")
    hx = lax.axis_index("head")
    z = me // 8
    y = lax.rem(me // 2, 4)
    a = lax.rem(me, 2)
    b = 1 - a
    me8 = lax.rem(me, 8)

    def at(zz, yy, cc):
        return (zz * 8 + yy * 2 + cc, hx)

    def zoff(d):
        return at(lax.rem(z + d + NZ, NZ), y, a)

    def yoff(d):
        return at(z, lax.rem(y + d, NY), a)

    def slaboff(d):
        return (z * 8 + lax.rem(me8 + d, 8), hx)

    def ctxoff(d):
        return (lax.rem(me + d + NCTX, NCTX), hx)

    sib = at(z, y, b)

    def remote(src, dst, ss, rs, dev):
        return pltpu.make_async_remote_copy(
            src_ref=src, dst_ref=dst, send_sem=ss, recv_sem=rs, device_id=dev, device_id_type=MESH
        )

    bar = pltpu.get_barrier_semaphore()
    peers = [zoff(d) for d in range(1, 8)] + [slaboff(d) for d in range(1, 8)]
    peers += [(me, lax.rem(hx + d, NX)) for d in range(1, NX)]
    peers += [ctxoff(d) for d in range(1, SPAN)] + [ctxoff(-d) for d in range(1, SPAN)]
    for dev in peers:
        pl.semaphore_signal(bar, inc=1, device_id=dev, device_id_type=MESH)
    pl.semaphore_wait(bar, len(peers))

    kv_in = (k_ref, v_ref)

    def cols(g):
        return pl.ds(pl.multiple_of(g * 128, 128), 128)

    local = []
    sib_kv = []
    ya = []
    for i in range(2):
        own = kv_in[i].at[:, cols(a)]
        local.append(pltpu.make_async_copy(own, kvb.at[i, z, y, a], loc_sem.at[i]))
        sib_kv.append(
            remote(kv_in[i].at[:, cols(b)], kvb.at[i, z, y, a], sib_s.at[i], sib_r.at[i], sib)
        )
        for d in range(1, NY):
            ya.append(
                remote(own, kvb.at[i, z, y, a], ya_s.at[i, d], ya_r.at[i, d], yoff(d))
            )
    sib_q = []
    for g in range(8):
        local.append(
            pltpu.make_async_copy(q_ref.at[:, cols(a * 8 + g)], qb.at[1, g], loc_sem.at[2 + g])
        )
        sib_q.append(
            remote(q_ref.at[:, cols(b * 8 + g)], qb.at[0, g], sib_s.at[2 + g], sib_r.at[2 + g], sib)
        )
    for c in sib_kv + ya + sib_q + local:
        c.start()

    def ring_a(i, p, sign):
        zz = lax.rem(z - sign * (p - 1) + 2 * NZ, NZ)
        blk = kvb.at[i, zz, :, a]
        k = 0 if sign > 0 else 1
        return remote(blk, blk, ra_s.at[i, k, p], ra_r.at[i, k, p], zoff(sign))

    def ring_b(i, p, sign):
        zz = lax.rem(z - sign * (p - 1) + 2 * NZ, NZ)
        blk = kvb.at[i, zz, y, b]
        k = 0 if sign > 0 else 1
        return remote(blk, blk, rb_s.at[i, k, p], rb_r.at[i, k, p], zoff(sign))

    def y_b(i, p, sign, d):
        zz = lax.rem(z - sign * p + 2 * NZ, NZ)
        blk = kvb.at[i, zz, y, b]
        k = 0 if sign > 0 else 1
        return remote(blk, blk, yb_s.at[i, k, p, d], yb_r.at[i, k, p, d], yoff(d))

    for i in range(2):
        sib_kv[i].wait_recv()
        ring_b(i, 1, 1).start()
        ring_b(i, 1, -1).start()
        for d in range(1, NY):
            y_b(i, 0, 1, d).start()

    for c in local:
        c.wait()
    for i in range(2):
        for d in range(1, NY):
            ya[i * 3 + d - 1].wait_recv()
        ring_a(i, 1, 1).start()
        ring_a(i, 1, -1).start()

    for d in range(SPAN):
        for h in range(2):
            kt = jnp.zeros((16, 128), F32)
            vt = jnp.zeros((16, 128), F32)
            for p in range(8):
                r = (d * 2 + h) * 8 + p
                w = w_ref[r : r + 1, :]
                kt += w * k_ref[p * 16 : (p + 1) * 16, h * 128 : (h + 1) * 128].astype(F32)
                vt += w * v_ref[p * 16 : (p + 1) * 16, h * 128 : (h + 1) * 128].astype(F32)
            tsend[d, h, 0:16, :] = kt.astype(BF16)
            tsend[d, h, 16:32, :] = vt.astype(BF16)
    pages = [None]
    for d in range(1, SPAN):
        pages.append(remote(tsend.at[d], trecv.at[d], pg_s.at[d], pg_r.at[d], ctxoff(d)))
        pages[d].start()

    for c in sib_q:
        c.wait_recv()
    run_m[...] = jnp.full_like(run_m, -1e30)
    run_l[...] = jnp.zeros_like(run_l)

    def fold(zz, masked):
        keys = kvb.at[0, zz]

        def tile(hc, carry):
            r = pl.ds(pl.multiple_of(hc * 1024, 1024), 1024)
            s = qk(
                qb[hc].reshape(1024, 128), keys[...].reshape(SLAB, 128)
            ) * SCALE2
            parts = [s[:, t * 128 : (t + 1) * 128] for t in range(LANES)]
            if masked:
                owner = lax.rem(a + 1 - hc + 2, 2)
                row = lax.broadcasted_iota(jnp.int32, (1024, 128), 0) % 128
                lane = lax.broadcasted_iota(jnp.int32, (1024, 128), 1)
                lim = row - lane + (y * 256 + owner * 128)
                parts = [jnp.where(lim >= t * 128, x, -1e30) for t, x in enumerate(parts)]
            m = run_m[r, :]
            top = functools.reduce(jnp.maximum, parts)
            mn = jnp.maximum(m, jnp.max(top, axis=1, keepdims=True))
            total = jnp.zeros((1024, 128), F32)
            for t in range(LANES):
                e = jnp.exp2(parts[t] - mn)
                total = total + e
                prob[zz, r, t * 128 : (t + 1) * 128] = e.astype(BF16)
            run_l[r, :] = run_l[r, :] * jnp.exp2(m - mn) + total
            run_m[r, :] = mn
            mx[zz, r, :] = mn
            return carry

        lax.fori_loop(0, 2, tile, 0)

    def phase(p, carry):
        @pl.when((p >= 1) & (p <= 4))
        def _():
            for i in range(2):
                ring_b(i, p, 1).wait_recv()

                @pl.when(p < 4)
                def _():
                    ring_b(i, p + 1, 1).start()
                    ring_b(i, p, -1).wait_recv()

                @pl.when(p < 3)
                def _():
                    ring_b(i, p + 1, -1).start()

                for d in range(1, NY):
                    y_b(i, p, 1, d).start()

                @pl.when(p < 4)
                def _():
                    for d in range(1, NY):
                        y_b(i, p, -1, d).start()

                ring_a(i, p, 1).wait_recv()

                @pl.when(p < 4)
                def _():
                    ring_a(i, p + 1, 1).start()
                    ring_a(i, p, -1).wait_recv()

                @pl.when(p < 3)
                def _():
                    ring_a(i, p + 1, -1).start()

        @pl.when(p >= 1)
        def _():
            pp = p - 1
            for i in range(2):
                for d in range(1, NY):
                    y_b(i, pp, 1, d).wait_recv()

                @pl.when((pp >= 1) & (pp < 4))
                def _():
                    for d in range(1, NY):
                        y_b(i, pp, -1, d).wait_recv()

            @pl.when(pp == 0)
            def _():
                fold(z, True)

            def side(j, c):
                up = j == 0
                zz = jnp.where(up, z - pp, z + pp - NZ)
                ok = (pp >= 1) & (zz >= 0) & (up | (pp < 4))

                @pl.when(ok)
                def _():
                    fold(zz, False)

                return c

            lax.fori_loop(0, 2, side, 0)

        return carry

    lax.fori_loop(0, 6, phase, 0)

    def finish(i, carry):
        r = pl.ds(pl.multiple_of(i * 256, 256), 256)
        lse = run_m[r, :] + jnp.log2(jnp.sum(run_l[r, :], axis=1, keepdims=True))

        def one(zz, c):
            mx[zz, r, :] = jnp.exp2(mx[zz, r, :] - lse)
            return c

        return lax.fori_loop(0, z + 1, one, carry)

    lax.fori_loop(0, ROWS // 256, finish, 0)

    csum[...] = jnp.zeros_like(csum)

    def colpass(zz, carry):
        def rows(i, c):
            r = pl.ds(pl.multiple_of(i * 256, 256), 256)
            w = mx[zz, r, :]
            out = []
            for t in range(LANES):
                x = prob[zz, r, t * 128 : (t + 1) * 128].astype(F32) * w
                out.append(c[t] + jnp.sum(x.reshape(32, 8, 128), axis=0))
            return tuple(out)

        c = lax.fori_loop(
            0, ROWS // 256, rows, tuple(jnp.zeros((8, 128), F32) for _ in range(LANES))
        )
        for t in range(LANES):
            csum[zz, t : t + 1, :] = jnp.sum(c[t], axis=0, keepdims=True)
        return carry

    lax.fori_loop(0, z + 1, colpass, 0)

    c1 = [None]
    for d in range(1, NZ):
        zz = lax.rem(z - d + NZ, NZ)
        c1.append(remote(csum.at[zz], csr.at[d], c1_s.at[d], c1_r.at[d], zoff(-d)))
        c1[d].start()

    def weigh(hc):
        r = slice(hc * 1024, (hc + 1) * 1024)
        acc[...] = jnp.zeros_like(acc)

        def one(zz, c):
            vals = kvb.at[1, zz][...].reshape(SLAB, 128)
            acc[...] += mx[zz, r, :] * jnp.dot(prob[zz, r, :], vals, preferred_element_type=F32)
            return c

        lax.fori_loop(0, z + 1, one, 0)

    weigh(0)
    outs = []
    for g in range(8):
        osend[g] = acc[g * 128 : (g + 1) * 128, :].astype(BF16)
        outs.append(
            remote(osend.at[g], att_ref.at[:, cols(a * 8 + g)], o_s.at[g], o_r.at[g], sib)
        )
        outs[g].start()

    total = csum[z]
    for d in range(1, NZ):
        c1[d].wait_recv()
        total = total + csr[d]
    for t in range(8):
        tot8[t] = jnp.broadcast_to(total[t : t + 1, :], (8, 128))
    c2 = [None]
    for d in range(1, 8):
        c2.append(
            remote(tot8.at[lax.rem(me8 + d, 8)], t2.at[d], c2_s.at[d], c2_r.at[d], slaboff(d))
        )
        c2[d].start()

    weigh(1)
    for g in range(8):
        att_ref[:, cols(a * 8 + g)] = acc[g * 128 : (g + 1) * 128, :].astype(BF16)

    same = tot8[me8]
    other = jnp.zeros((8, 128), F32)
    for d in range(1, 8):
        c2[d].wait_recv()
        if d % 2 == 0:
            same = same + t2[d]
        else:
            other = other + t2[d]
    lane = lax.broadcasted_iota(jnp.int32, (8, 128), 1)
    sub = lax.broadcasted_iota(jnp.int32, (8, 128), 0)
    pos = me * BLK + lane
    factor = (NCTX * BLK / 8.0) / (NCTX * BLK - pos).astype(F32)
    col = [jnp.where(a == 0, same, other) * factor, jnp.where(a == 0, other, same) * factor]
    impb[...] = col[0] + col[1]
    im = [None]
    for d in range(1, NX):
        im.append(
            remote(impb, impr.at[d], im_s.at[d], im_r.at[d], (me, lax.rem(hx + d, NX)))
        )
        im[d].start()
    means = [
        jnp.sum(jnp.where(lane // 16 == sub, c, 0.0), axis=1, keepdims=True) / 16.0 for c in col
    ]
    for d in range(SPAN):
        for h in range(2):
            r = (d * 2 + h) * 8
            ssend[d, h : h + 1, :] = jnp.sum(w_ref[r : r + 8, :] * means[h], axis=0, keepdims=True)
    sc = [None]
    for d in range(1, SPAN):
        sc.append(remote(ssend.at[d], srecv.at[d], sc_s.at[d], sc_r.at[d], ctxoff(d)))
        sc[d].start()

    for d in range(1, SPAN):
        pages[d].wait_recv()
    for h in range(2):
        for slot in range(8):
            kt = jnp.zeros((16, 128), F32)
            vt = jnp.zeros((16, 128), F32)
            for d in range(SPAN):
                r = (d * 2 + h) * 8 + slot
                w = r_ref[r : r + 1, :]
                src = tsend if d == 0 else trecv
                kt += w * src[d, h, 0:16, :].astype(F32)
                vt += w * src[d, h, 16:32, :].astype(F32)
            for n, x in enumerate((kt, vt)):
                amax = jnp.max(jnp.max(jnp.abs(x), axis=0, keepdims=True), axis=1, keepdims=True)
                tile_ref[h, slot, n * 16 : (n + 1) * 16, :] = (x * 7.0 / (amax + 1e-6)).astype(BF16)
                scale_ref[h, slot, n : n + 1, :] = jnp.broadcast_to(amax / 7.0, (1, 128))
            bound_ref[h, slot, 0:1, :] = jnp.min(kt, axis=0, keepdims=True)
            bound_ref[h, slot, 1:2, :] = jnp.max(kt, axis=0, keepdims=True)

    for d in range(1, SPAN):
        sc[d].wait_recv()
    for h in range(2):
        got = jnp.zeros((8, 128), F32)
        for d in range(SPAN):
            r = (d * 2 + h) * 8
            src = ssend if d == 0 else srecv
            got += r_ref[r : r + 8, :] * src[d, h : h + 1, :]
        score_ref[h] = got
    imp = impb[...]
    for d in range(1, NX):
        im[d].wait_recv()
        imp = imp + impr[d]
    imp_ref[...] = imp

    for g in range(8):
        outs[g].wait()
    for c in sib_kv + ya + sib_q:
        c.wait_send()
    for i in range(2):
        for d in range(1, NY):
            y_b(i, 0, 1, d).wait_send()
        for p in range(1, 5):
            signs = (1, -1) if p < 4 else (1,)
            for s in signs:
                ring_a(i, p, s).wait_send()
                ring_b(i, p, s).wait_send()
                for d in range(1, NY):
                    y_b(i, p, s, d).wait_send()
    for group in (pages, c1, c2, im, sc):
        for c in group[1:]:
            c.wait_send()


def on_device(queries, key_states, value_states, keep_pages, keep_count, dest_slot):
    vmem = pl.BlockSpec(memory_space=pltpu.VMEM)
    smem = pl.BlockSpec(memory_space=pltpu.SMEM)
    table = jax.ShapeDtypeStruct((128, 128), F32)
    picks = pl.pallas_call(
        picks_kernel,
        out_shape=[table, table],
        in_specs=[smem] * 3,
        out_specs=[vmem] * 2,
    )
    w, r = picks(keep_pages, keep_count, dest_slot)
    dma = pltpu.SemaphoreType.DMA
    call = pl.pallas_call(
        main_kernel,
        out_shape=[
            jax.ShapeDtypeStruct((BLK, 2048), BF16),
            jax.ShapeDtypeStruct((8, 128), F32),
            jax.ShapeDtypeStruct((2, 8, 32, 128), BF16),
            jax.ShapeDtypeStruct((2, 8, 2, 128), F32),
            jax.ShapeDtypeStruct((2, 8, 2, 128), F32),
            jax.ShapeDtypeStruct((2, 8, 128), F32),
        ],
        in_specs=[vmem] * 5,
        out_specs=[vmem] * 6,
        scratch_shapes=[
            pltpu.VMEM((2, 8, BLK, 128), BF16),
            pltpu.VMEM((2, NZ, NY, NC, BLK, 128), BF16),
            pltpu.VMEM((NZ, ROWS, SLAB), BF16),
            pltpu.VMEM((NZ, ROWS, 128), F32),
            pltpu.VMEM((ROWS, 128), F32),
            pltpu.VMEM((ROWS, 128), F32),
            pltpu.VMEM((ROWS // 2, 128), F32),
            pltpu.VMEM((8, BLK, 128), BF16),
            pltpu.VMEM((NZ, 8, 128), F32),
            pltpu.VMEM((NZ, 8, 128), F32),
            pltpu.VMEM((8, 8, 128), F32),
            pltpu.VMEM((8, 8, 128), F32),
            pltpu.VMEM((8, 128), F32),
            pltpu.VMEM((NX, 8, 128), F32),
            pltpu.VMEM((SPAN, 2, 32, 128), BF16),
            pltpu.VMEM((SPAN, 2, 32, 128), BF16),
            pltpu.VMEM((SPAN, 8, 128), F32),
            pltpu.VMEM((SPAN, 8, 128), F32),
            dma((10,)),
            dma((10,)), dma((10,)),
            dma((2, NY)), dma((2, NY)),
            dma((2, 2, 5, NY)), dma((2, 2, 5, NY)),
            dma((2, 2, 5)), dma((2, 2, 5)),
            dma((2, 2, 5)), dma((2, 2, 5)),
            dma((SPAN,)), dma((SPAN,)),
            dma((NZ,)), dma((NZ,)),
            dma((8,)), dma((8,)),
            dma((NX,)), dma((NX,)),
            dma((SPAN,)), dma((SPAN,)),
            dma((8,)), dma((8,)),
        ],
        compiler_params=pltpu.CompilerParams(
            collective_id=0, has_side_effects=True, vmem_limit_bytes=62 * 2**20
        ),
    )
    att, imp, tiles, scale, bound, score = call(queries, key_states, value_states, w, r)
    return (
        att,
        imp[0],
        tiles.reshape(1, 2, 8, 4096),
        scale[None, :, :, :, 0],
        bound[None],
        score[None, :, :, 0],
    )


def solution(mesh):
    in_specs = (
        P("ctx", "head"),
        P("ctx", "head"),
        P("ctx", "head"),
        P("head", "ctx", None),
        P("head", None),
        P("head", None, None),
    )
    out_specs = (
        P("ctx", "head"),
        P("ctx"),
        P("ctx", "head", None, None),
        P("ctx", "head", None, None),
        P("ctx", "head", None, None, None),
        P("ctx", "head", None),
    )
    return jax.shard_map(
        on_device, mesh=mesh, in_specs=in_specs, out_specs=out_specs, check_vma=False
    )
```

```python
import functools

import jax
import jax.numpy as jnp
from jax import lax
from jax.experimental import pallas as pl
from jax.experimental.pallas import tpu as pltpu
from jax.sharding import PartitionSpec as P

MESH = pl.DeviceIdType.MESH
F32 = jnp.float32
BF16 = jnp.bfloat16
NZ, NY, NC, NX = 8, 4, 2, 4
NCTX = NZ * NY * NC
BLK = 128
SLAB = NY * NC * BLK
ROWS = 2 * 8 * BLK
SPAN = 8
SCALE2 = 1.4426950408889634 / 128.0**0.5
LANES = SLAB // 128


def qk(a, b):
    return lax.dot_general(a, b, (((1,), (1,)), ((), ())), preferred_element_type=F32)


def main_kernel(
    q_ref, k_ref, v_ref, pages_ref, count_ref, slot_ref,
    att_ref, imp_ref, tile_ref, scale_ref, bound_ref, score_ref,
    w_ref, r_ref, qb, kvb, prob, mx, run_m, run_l, acc, osend, csum, csr, tot8, t2, impb, impr, tsend, trecv,
    ssend, srecv, loc_sem, sib_s, sib_r, ya_s, ya_r, yb_s, yb_r, ra_s, ra_r, rb_s, rb_r,
    pg_s, pg_r, c1_s, c1_r, c2_s, c2_r, im_s, im_r, sc_s, sc_r, o_s, o_r,
):
    me = lax.axis_index("ctx")
    hx = lax.axis_index("head")
    z = me // 8
    y = lax.rem(me // 2, 4)
    a = lax.rem(me, 2)
    b = 1 - a
    me8 = lax.rem(me, 8)

    def at(zz, yy, cc):
        return (zz * 8 + yy * 2 + cc, hx)

    def zoff(d):
        return at(lax.rem(z + d + NZ, NZ), y, a)

    def yoff(d):
        return at(z, lax.rem(y + d, NY), a)

    def slaboff(d):
        return (z * 8 + lax.rem(me8 + d, 8), hx)

    def ctxoff(d):
        return (lax.rem(me + d + NCTX, NCTX), hx)

    sib = at(z, y, b)

    def remote(src, dst, ss, rs, dev):
        return pltpu.make_async_remote_copy(
            src_ref=src, dst_ref=dst, send_sem=ss, recv_sem=rs, device_id=dev, device_id_type=MESH
        )

    bar = pltpu.get_barrier_semaphore()
    peers = [zoff(d) for d in range(1, 8)] + [slaboff(d) for d in range(1, 8)]
    peers += [(me, lax.rem(hx + d, NX)) for d in range(1, NX)]
    peers += [ctxoff(d) for d in range(1, SPAN)] + [ctxoff(-d) for d in range(1, SPAN)]
    for dev in peers:
        pl.semaphore_signal(bar, inc=1, device_id=dev, device_id_type=MESH)
    pl.semaphore_wait(bar, len(peers))

    kv_in = (k_ref, v_ref)

    def cols(g):
        return pl.ds(pl.multiple_of(g * 128, 128), 128)

    local = []
    sib_kv = []
    ya = []
    for i in range(2):
        own = kv_in[i].at[:, cols(a)]
        local.append(pltpu.make_async_copy(own, kvb.at[i, z, y, a], loc_sem.at[i]))
        sib_kv.append(
            remote(kv_in[i].at[:, cols(b)], kvb.at[i, z, y, a], sib_s.at[i], sib_r.at[i], sib)
        )
        for d in range(1, NY):
            ya.append(
                remote(own, kvb.at[i, z, y, a], ya_s.at[i, d], ya_r.at[i, d], yoff(d))
            )
    sib_q = []
    for g in range(8):
        local.append(
            pltpu.make_async_copy(q_ref.at[:, cols(a * 8 + g)], qb.at[1, g], loc_sem.at[2 + g])
        )
        sib_q.append(
            remote(q_ref.at[:, cols(b * 8 + g)], qb.at[0, g], sib_s.at[2 + g], sib_r.at[2 + g], sib)
        )
    for c in [sib_kv[0]] + ya[:3] + sib_q + [sib_kv[1]] + local:
        c.start()

    def ring_a(i, p, sign):
        zz = lax.rem(z - sign * (p - 1) + 2 * NZ, NZ)
        blk = kvb.at[i, zz, :, a]
        k = 0 if sign > 0 else 1
        return remote(blk, blk, ra_s.at[i, k, p], ra_r.at[i, k, p], zoff(sign))

    def ring_b(i, p, sign):
        zz = lax.rem(z - sign * (p - 1) + 2 * NZ, NZ)
        blk = kvb.at[i, zz, y, b]
        k = 0 if sign > 0 else 1
        return remote(blk, blk, rb_s.at[i, k, p], rb_r.at[i, k, p], zoff(sign))

    def y_b(i, p, sign, d):
        zz = lax.rem(z - sign * p + 2 * NZ, NZ)
        blk = kvb.at[i, zz, y, b]
        k = 0 if sign > 0 else 1
        return remote(blk, blk, yb_s.at[i, k, p, d], yb_r.at[i, k, p, d], yoff(d))

    def begin_b(i):
        sib_kv[i].wait_recv()
        ring_b(i, 1, 1).start()
        ring_b(i, 1, -1).start()
        for d in range(1, NY):
            y_b(i, 0, 1, d).start()

    def begin_a(i):
        for d in range(1, NY):
            ya[i * 3 + d - 1].wait_recv()
        ring_a(i, 1, 1).start()
        ring_a(i, 1, -1).start()

    begin_b(0)
    for c in local:
        c.wait()
    begin_a(0)

    sub8 = lax.broadcasted_iota(jnp.int32, (8, 8), 0)
    lane8 = lax.broadcasted_iota(jnp.int32, (8, 8), 1)
    lane64 = lax.broadcasted_iota(jnp.int32, (1, 64), 1)
    lane864 = lax.broadcasted_iota(jnp.int32, (8, 64), 1)

    def kept(h, src):
        row = jnp.where(lane64 == src, count_ref[h : h + 1, :].astype(F32), 0.0)
        return lane8.astype(F32) < jnp.sum(row, axis=1, keepdims=True)

    def spread(hit):
        return jnp.broadcast_to(
            jnp.sum(jnp.where(hit, 1.0, 0.0), axis=1, keepdims=True), (8, 128)
        )

    def slot_row(h, src):
        col = jnp.sum(
            jnp.where(lane864 == src, slot_ref[h].astype(F32), 0.0), axis=1, keepdims=True
        )
        row = jnp.sum(jnp.where(sub8 == lane8, col, 0.0), axis=0, keepdims=True)
        return row.astype(jnp.int32)

    for h in range(2):
        slots = slot_row(h, me)
        off = ((slots >> 3) - me) & (NCTX - 1)
        base = (pages_ref[h, 0:1, :] == sub8) & kept(h, me)
        for d in range(SPAN):
            r = (d * 2 + h) * 8
            w_ref[r : r + 8, :] = spread(base & (off == d))
            src = lax.rem(me - d + NCTX, NCTX)
            slots = slot_row(h, src)
            hit = ((slots >> 3) == me) & ((slots & 7) == sub8) & kept(h, src)
            r_ref[r : r + 8, :] = spread(hit)

    for d in range(SPAN):
        for h in range(2):
            kt = jnp.zeros((16, 128), F32)
            vt = jnp.zeros((16, 128), F32)
            for p in range(8):
                r = (d * 2 + h) * 8 + p
                w = w_ref[r : r + 1, :]
                kt += w * k_ref[p * 16 : (p + 1) * 16, h * 128 : (h + 1) * 128].astype(F32)
                vt += w * v_ref[p * 16 : (p + 1) * 16, h * 128 : (h + 1) * 128].astype(F32)
            tsend[d, h, 0:16, :] = kt.astype(BF16)
            tsend[d, h, 16:32, :] = vt.astype(BF16)
    pages = [None]
    for d in range(1, SPAN):
        pages.append(remote(tsend.at[d], trecv.at[d], pg_s.at[d], pg_r.at[d], ctxoff(d)))
        pages[d].start()

    for c in sib_q:
        c.wait_recv()
    run_m[...] = jnp.full_like(run_m, -1e30)
    run_l[...] = jnp.zeros_like(run_l)

    def fold(zz, masked):
        keys = kvb.at[0, zz]

        def tile(n, carry):
            hc = n // 2
            r = pl.ds(n * 512, 512)
            s = qk(
                qb[hc, (n % 2) * 4 : (n % 2) * 4 + 4].reshape(512, 128),
                keys[...].reshape(SLAB, 128),
            ) * SCALE2
            parts = [s[:, t * 128 : (t + 1) * 128] for t in range(LANES)]
            if masked:
                owner = lax.rem(a + 1 - hc + 2, 2)
                row = lax.broadcasted_iota(jnp.int32, (512, 128), 0) % 128
                lane = lax.broadcasted_iota(jnp.int32, (512, 128), 1)
                lim = row - lane + (y * 256 + owner * 128)
                parts = [jnp.where(lim >= t * 128, x, -1e30) for t, x in enumerate(parts)]
            m = run_m[r, :]
            top = functools.reduce(jnp.maximum, parts)
            mn = jnp.maximum(m, jnp.max(top, axis=1, keepdims=True))
            total = jnp.zeros((512, 128), F32)
            for t in range(LANES):
                e = jnp.exp2(parts[t] - mn)
                total = total + e
                prob[zz, r, t * 128 : (t + 1) * 128] = e.astype(BF16)
            run_l[r, :] = run_l[r, :] * jnp.exp2(m - mn) + total
            run_m[r, :] = mn
            mx[zz, r, :] = mn
            return carry

        for n in range(4):
            tile(n, 0)

    def hop(i, p):
        p = jnp.int32(p)
        ring_b(i, p, 1).wait_recv()

        @pl.when(p < 4)
        def _():
            ring_b(i, p + 1, 1).start()
            ring_b(i, p, -1).wait_recv()

        @pl.when(p < 3)
        def _():
            ring_b(i, p + 1, -1).start()

        for d in range(1, NY):
            y_b(i, p, 1, d).start()

        @pl.when(p < 4)
        def _():
            for d in range(1, NY):
                y_b(i, p, -1, d).start()

        ring_a(i, p, 1).wait_recv()

        @pl.when(p < 4)
        def _():
            ring_a(i, p + 1, 1).start()
            ring_a(i, p, -1).wait_recv()

        @pl.when(p < 3)
        def _():
            ring_a(i, p + 1, -1).start()

    def landed(i, p):
        for d in range(1, NY):
            y_b(i, p, 1, d).wait_recv()

        @pl.when((p >= 1) & (p < 4))
        def _():
            for d in range(1, NY):
                y_b(i, p, -1, d).wait_recv()

    def phase(p, carry):
        @pl.when(p <= 4)
        def _():
            hop(0, p)

        @pl.when(p == 1)
        def _():
            for c in ya[3:]:
                c.start()

        @pl.when(p == 2)
        def _():
            begin_b(1)
            begin_a(1)

        pp = p - 1
        landed(0, pp)

        if True:
            @pl.when(pp == 0)
            def _():
                fold(z, True)

            def side(j, c):
                up = j == 0
                zz = jnp.where(up, z - pp, z + pp - NZ)
                ok = (pp >= 1) & (zz >= 0) & (up | (pp < 4))

                @pl.when(ok)
                def _():
                    fold(zz, False)

                return c

            lax.fori_loop(0, 2, side, 0)

        @pl.when(p >= 3)
        def _():
            hop(1, p - 2)

        return carry

    lax.fori_loop(1, 6, phase, 0)

    run_m[...] = run_m[...] + jnp.log2(jnp.sum(run_l[...], axis=1, keepdims=True))
    csum[...] = jnp.zeros_like(csum)

    def colpass(zz, carry):
        def rows(i, c):
            r = pl.ds(pl.multiple_of(i * 256, 256), 256)
            w = jnp.exp2(mx[zz, r, :] - run_m[r, :])
            mx[zz, r, :] = w
            out = []
            for t in range(LANES):
                x = prob[zz, r, t * 128 : (t + 1) * 128].astype(F32) * w
                out.append(c[t] + jnp.sum(x.reshape(32, 8, 128), axis=0))
            return tuple(out)

        c = lax.fori_loop(
            0, ROWS // 256, rows, tuple(jnp.zeros((8, 128), F32) for _ in range(LANES))
        )
        for t in range(LANES):
            csum[zz, t : t + 1, :] = jnp.sum(c[t], axis=0, keepdims=True)
        return carry

    half = (z + 1) // 2
    lax.fori_loop(0, half, colpass, 0)
    hop(1, 4)
    lax.fori_loop(half, z + 1, colpass, 0)

    c1 = [None]
    for d in range(1, NZ):
        zz = lax.rem(z - d + NZ, NZ)
        c1.append(remote(csum.at[zz], csr.at[d], c1_s.at[d], c1_r.at[d], zoff(-d)))
        c1[d].start()

    lax.fori_loop(0, 5, lambda p, c: (landed(1, p), c)[1], 0)

    def weigh(hc):
        r = slice(hc * 1024, (hc + 1) * 1024)
        acc[...] = jnp.zeros_like(acc)

        def one(zz, c):
            vals = kvb.at[1, zz][...].reshape(SLAB, 128)
            acc[...] += mx[zz, r, :] * jnp.dot(prob[zz, r, :], vals, preferred_element_type=F32)
            return c

        lax.fori_loop(0, z + 1, one, 0)

    weigh(0)
    outs = []
    for g in range(8):
        osend[g] = acc[g * 128 : (g + 1) * 128, :].astype(BF16)
        outs.append(
            remote(osend.at[g], att_ref.at[:, cols(a * 8 + g)], o_s.at[g], o_r.at[g], sib)
        )
        outs[g].start()

    total = csum[z]
    for d in range(1, NZ):
        c1[d].wait_recv()
        total = total + csr[d]
    for t in range(8):
        tot8[t] = jnp.broadcast_to(total[t : t + 1, :], (8, 128))
    c2 = [None]
    for d in range(1, 8):
        c2.append(
            remote(tot8.at[lax.rem(me8 + d, 8)], t2.at[d], c2_s.at[d], c2_r.at[d], slaboff(d))
        )
        c2[d].start()

    weigh(1)
    for g in range(8):
        att_ref[:, cols(a * 8 + g)] = acc[g * 128 : (g + 1) * 128, :].astype(BF16)

    same = tot8[me8]
    other = jnp.zeros((8, 128), F32)
    for d in range(1, 8):
        c2[d].wait_recv()
        if d % 2 == 0:
            same = same + t2[d]
        else:
            other = other + t2[d]
    lane = lax.broadcasted_iota(jnp.int32, (8, 128), 1)
    sub = lax.broadcasted_iota(jnp.int32, (8, 128), 0)
    pos = me * BLK + lane
    factor = (NCTX * BLK / 8.0) / (NCTX * BLK - pos).astype(F32)
    col = [jnp.where(a == 0, same, other) * factor, jnp.where(a == 0, other, same) * factor]
    impb[...] = col[0] + col[1]
    im = [None]
    for d in range(1, NX):
        im.append(
            remote(impb, impr.at[d], im_s.at[d], im_r.at[d], (me, lax.rem(hx + d, NX)))
        )
        im[d].start()
    means = [
        jnp.sum(jnp.where(lane // 16 == sub, c, 0.0), axis=1, keepdims=True) / 16.0 for c in col
    ]
    for d in range(SPAN):
        for h in range(2):
            r = (d * 2 + h) * 8
            ssend[d, h : h + 1, :] = jnp.sum(w_ref[r : r + 8, :] * means[h], axis=0, keepdims=True)
    sc = [None]
    for d in range(1, SPAN):
        sc.append(remote(ssend.at[d], srecv.at[d], sc_s.at[d], sc_r.at[d], ctxoff(d)))
        sc[d].start()

    for d in range(1, SPAN):
        pages[d].wait_recv()
    for h in range(2):
        got = [
            (tsend if d == 0 else trecv)[d, h].astype(F32) for d in range(SPAN)
        ]
        place = [r_ref[(d * 2 + h) * 8 : (d * 2 + h) * 8 + 8, :] for d in range(SPAN)]
        scales = []
        for n in range(2):
            rows = [
                functools.reduce(
                    jnp.add, [place[d] * got[d][t : t + 1, :] for d in range(SPAN)]
                )
                for t in range(n * 16, n * 16 + 16)
            ]
            big = functools.reduce(jnp.maximum, [jnp.abs(x) for x in rows])
            amax = jnp.max(big, axis=1, keepdims=True)
            scales.append(amax / 7.0)
            for t, x in enumerate(rows):
                c = (n * 16 + t) * 128
                tile_ref[0, h, :, c : c + 128] = (x * 7.0 / (amax + 1e-6)).astype(BF16)
            if n == 0:
                low = functools.reduce(jnp.minimum, rows)
                high = functools.reduce(jnp.maximum, rows)
                for slot in range(8):
                    bound_ref[0, h, slot, 0:1, :] = low[slot : slot + 1, :]
                    bound_ref[0, h, slot, 1:2, :] = high[slot : slot + 1, :]
        for n in range(2):
            row = jnp.sum(jnp.where(lane == sub, scales[n], 0.0), axis=0, keepdims=True)
            scale_ref[0, h, n : n + 1, :] = row[:, 0:8]

    for d in range(1, SPAN):
        sc[d].wait_recv()
    for h in range(2):
        got = jnp.zeros((8, 128), F32)
        for d in range(SPAN):
            r = (d * 2 + h) * 8
            src = ssend if d == 0 else srecv
            got += r_ref[r : r + 8, :] * src[d, h : h + 1, :]
        row = jnp.sum(jnp.where(lane == sub, got, 0.0), axis=0, keepdims=True)
        score_ref[0, h : h + 1, :] = row[:, 0:8]
    imp = impb[...]
    for d in range(1, NX):
        im[d].wait_recv()
        imp = imp + impr[d]
    imp_ref[...] = imp[0:1, :]

    for g in range(8):
        outs[g].wait()
    for c in sib_kv + ya + sib_q:
        c.wait_send()
    for i in range(2):
        for d in range(1, NY):
            y_b(i, 0, 1, d).wait_send()
        for p in range(1, 5):
            signs = (1, -1) if p < 4 else (1,)
            for s in signs:
                ring_a(i, p, s).wait_send()
                ring_b(i, p, s).wait_send()
                for d in range(1, NY):
                    y_b(i, p, s, d).wait_send()
    for group in (pages, c1, c2, im, sc):
        for c in group[1:]:
            c.wait_send()


def hand_over_kernel(*refs):
    for i in range(6):
        refs[6 + i][...] = refs[i][...]


def on_device(queries, key_states, value_states, keep_pages, keep_count, dest_slot):
    vmem = pl.BlockSpec(memory_space=pltpu.VMEM)
    dma = pltpu.SemaphoreType.DMA
    call = pl.pallas_call(
        main_kernel,
        out_shape=[
            jax.ShapeDtypeStruct((BLK, 2048), BF16),
            jax.ShapeDtypeStruct((1, 128), F32),
            jax.ShapeDtypeStruct((1, 2, 8, 4096), BF16),
            jax.ShapeDtypeStruct((1, 2, 2, 8), F32),
            jax.ShapeDtypeStruct((1, 2, 8, 2, 128), F32),
            jax.ShapeDtypeStruct((1, 2, 8), F32),
        ],
        in_specs=[vmem] * 6,
        out_specs=[vmem] * 6,
        scratch_shapes=[
            pltpu.VMEM((128, 128), F32),
            pltpu.VMEM((128, 128), F32),
            pltpu.VMEM((2, 8, BLK, 128), BF16),
            pltpu.VMEM((2, NZ, NY, NC, BLK, 128), BF16),
            pltpu.VMEM((NZ, ROWS, SLAB), BF16),
            pltpu.VMEM((NZ, ROWS, 128), F32),
            pltpu.VMEM((ROWS, 128), F32),
            pltpu.VMEM((ROWS, 128), F32),
            pltpu.VMEM((ROWS // 2, 128), F32),
            pltpu.VMEM((8, BLK, 128), BF16),
            pltpu.VMEM((NZ, 8, 128), F32),
            pltpu.VMEM((NZ, 8, 128), F32),
            pltpu.VMEM((8, 8, 128), F32),
            pltpu.VMEM((8, 8, 128), F32),
            pltpu.VMEM((8, 128), F32),
            pltpu.VMEM((NX, 8, 128), F32),
            pltpu.VMEM((SPAN, 2, 32, 128), BF16),
            pltpu.VMEM((SPAN, 2, 32, 128), BF16),
            pltpu.VMEM((SPAN, 8, 128), F32),
            pltpu.VMEM((SPAN, 8, 128), F32),
            dma((10,)),
            dma((10,)), dma((10,)),
            dma((2, NY)), dma((2, NY)),
            dma((2, 2, 5, NY)), dma((2, 2, 5, NY)),
            dma((2, 2, 5)), dma((2, 2, 5)),
            dma((2, 2, 5)), dma((2, 2, 5)),
            dma((SPAN,)), dma((SPAN,)),
            dma((NZ,)), dma((NZ,)),
            dma((8,)), dma((8,)),
            dma((NX,)), dma((NX,)),
            dma((SPAN,)), dma((SPAN,)),
            dma((8,)), dma((8,)),
        ],
        compiler_params=pltpu.CompilerParams(
            collective_id=0, has_side_effects=True, vmem_limit_bytes=62 * 2**20
        ),
    )
    slots = jnp.transpose(dest_slot, (0, 2, 1))
    made = call(queries, key_states, value_states, keep_pages, keep_count, slots)
    hand_over = pl.pallas_call(
        hand_over_kernel,
        out_shape=[jax.ShapeDtypeStruct(x.shape, x.dtype) for x in made],
        in_specs=[vmem] * 6,
        out_specs=[vmem] * 6,
    )
    att, imp, tiles, scale, bound, score = hand_over(*made)
    return (att, imp[0], tiles, jnp.transpose(scale, (0, 1, 3, 2)), bound, score)


def solution(mesh):
    in_specs = (
        P("ctx", "head"),
        P("ctx", "head"),
        P("ctx", "head"),
        P("head", "ctx", None),
        P("head", None),
        P("head", None, None),
    )
    out_specs = (
        P("ctx", "head"),
        P("ctx"),
        P("ctx", "head", None, None),
        P("ctx", "head", None, None),
        P("ctx", "head", None, None, None),
        P("ctx", "head", None),
    )
    return jax.shard_map(
        on_device, mesh=mesh, in_specs=in_specs, out_specs=out_specs, check_vma=False
    )
```

```python
import functools

import jax
import jax.numpy as jnp
from jax import lax
from jax.experimental import pallas as pl
from jax.experimental.pallas import tpu as pltpu
from jax.sharding import PartitionSpec as P

MESH = pl.DeviceIdType.MESH
F32 = jnp.float32
BF16 = jnp.bfloat16
NZ, NY, NC, NX = 8, 4, 2, 4
NCTX = NZ * NY * NC
BLK = 128
SLAB = NY * NC * BLK
ROWS = 2 * 8 * BLK
SPAN = 8
SCALE2 = 1.4426950408889634 / 128.0**0.5
LANES = SLAB // 128


def qk(a, b):
    return lax.dot_general(a, b, (((1,), (1,)), ((), ())), preferred_element_type=F32)


def main_kernel(
    q_ref, k_ref, v_ref, pages_ref, count_ref, slot_ref,
    att_ref, imp_ref, tile_ref, scale_ref, bound_ref, score_ref,
    w_ref, r_ref, qb, q2, kvb, prob, mx, run_m, run_l, acc, osend, csum, csr, tot8, t2, impb, impr, tsend, trecv,
    ssend, srecv, loc_sem, sib_s, sib_r, ya_s, ya_r, yb_s, yb_r, ra_s, ra_r, rb_s, rb_r,
    pg_s, pg_r, c1_s, c1_r, c2_s, c2_r, im_s, im_r, sc_s, sc_r, o_s, o_r,
):
    me = lax.axis_index("ctx")
    hx = lax.axis_index("head")
    z = me // 8
    y = lax.rem(me // 2, 4)
    a = lax.rem(me, 2)
    b = 1 - a
    me8 = lax.rem(me, 8)

    def at(zz, yy, cc):
        return (zz * 8 + yy * 2 + cc, hx)

    def zoff(d):
        return at(lax.rem(z + d + NZ, NZ), y, a)

    def yoff(d):
        return at(z, lax.rem(y + d, NY), a)

    def slaboff(d):
        return (z * 8 + lax.rem(me8 + d, 8), hx)

    def ctxoff(d):
        return (lax.rem(me + d + NCTX, NCTX), hx)

    sib = at(z, y, b)

    def remote(src, dst, ss, rs, dev):
        return pltpu.make_async_remote_copy(
            src_ref=src, dst_ref=dst, send_sem=ss, recv_sem=rs, device_id=dev, device_id_type=MESH
        )

    bar = pltpu.get_barrier_semaphore()
    peers = [zoff(d) for d in range(1, 8)] + [slaboff(d) for d in range(1, 8)]
    peers += [(me, lax.rem(hx + d, NX)) for d in range(1, NX)]
    peers += [ctxoff(d) for d in range(1, SPAN)] + [ctxoff(-d) for d in range(1, SPAN)]
    for dev in peers:
        pl.semaphore_signal(bar, inc=1, device_id=dev, device_id_type=MESH)
    pl.semaphore_wait(bar, len(peers))

    kv_in = (k_ref, v_ref)

    def cols(g):
        return pl.ds(pl.multiple_of(g * 128, 128), 128)

    local = []
    sib_kv = []
    ya = []
    for i in range(2):
        own = kv_in[i].at[:, cols(a)]
        local.append(pltpu.make_async_copy(own, kvb.at[i, z, y, a], loc_sem.at[i]))
        sib_kv.append(
            remote(kv_in[i].at[:, cols(b)], kvb.at[i, z, y, a], sib_s.at[i], sib_r.at[i], sib)
        )
        for d in range(1, NY):
            ya.append(
                remote(own, kvb.at[i, z, y, a], ya_s.at[i, d], ya_r.at[i, d], yoff(d))
            )
    sib_q = []
    for g in range(8):
        local.append(
            pltpu.make_async_copy(q_ref.at[:, cols(a * 8 + g)], qb.at[1, g], loc_sem.at[2 + g])
        )
        sib_q.append(
            remote(q_ref.at[:, cols(b * 8 + g)], qb.at[0, g], sib_s.at[2 + g], sib_r.at[2 + g], sib)
        )
    for c in [sib_kv[0]] + local + ya[:3] + sib_q + [sib_kv[1]]:
        c.start()

    def ring_a(i, p, sign, e):
        zz = lax.rem(z - sign * (p - 1) + 2 * NZ, NZ)
        blk = kvb.at[i, zz, lax.rem(y + e, NY), a]
        k = 0 if sign > 0 else 1
        return remote(blk, blk, ra_s.at[i, k, p, e], ra_r.at[i, k, p, e], zoff(sign))

    def ring_b(i, p, sign):
        zz = lax.rem(z - sign * (p - 1) + 2 * NZ, NZ)
        blk = kvb.at[i, zz, y, b]
        k = 0 if sign > 0 else 1
        return remote(blk, blk, rb_s.at[i, k, p], rb_r.at[i, k, p], zoff(sign))

    def y_b(i, p, sign, d):
        zz = lax.rem(z - sign * p + 2 * NZ, NZ)
        blk = kvb.at[i, zz, y, b]
        k = 0 if sign > 0 else 1
        return remote(blk, blk, yb_s.at[i, k, p, d], yb_r.at[i, k, p, d], yoff(d))

    def begin_b(i):
        sib_kv[i].wait_recv()
        ring_b(i, 1, 1).start()
        ring_b(i, 1, -1).start()
        for d in range(1, NY):
            y_b(i, 0, 1, d).start()

    def begin_own(i):
        local[i].wait()
        ring_a(i, 1, 1, 0).start()
        ring_a(i, 1, -1, 0).start()

    def begin_a(i):
        for d in range(1, NY):
            ya[i * 3 + NY - d - 1].wait_recv()
            ring_a(i, 1, 1, d).start()
            ring_a(i, 1, -1, d).start()

    begin_own(0)
    begin_b(0)
    for c in local[2:]:
        c.wait()
    begin_a(0)

    sub8 = lax.broadcasted_iota(jnp.int32, (8, 8), 0)
    lane8 = lax.broadcasted_iota(jnp.int32, (8, 8), 1)
    lane64 = lax.broadcasted_iota(jnp.int32, (1, 64), 1)
    lane864 = lax.broadcasted_iota(jnp.int32, (8, 64), 1)

    def kept(h, src):
        row = jnp.where(lane64 == src, count_ref[h : h + 1, :].astype(F32), 0.0)
        return lane8.astype(F32) < jnp.sum(row, axis=1, keepdims=True)

    def spread(hit):
        return jnp.broadcast_to(
            jnp.sum(jnp.where(hit, 1.0, 0.0), axis=1, keepdims=True), (8, 128)
        )

    def slot_row(h, src):
        col = jnp.sum(
            jnp.where(lane864 == src, slot_ref[h].astype(F32), 0.0), axis=1, keepdims=True
        )
        row = jnp.sum(jnp.where(sub8 == lane8, col, 0.0), axis=0, keepdims=True)
        return row.astype(jnp.int32)

    for h in range(2):
        slots = slot_row(h, me)
        off = ((slots >> 3) - me) & (NCTX - 1)
        base = (pages_ref[h, 0:1, :] == sub8) & kept(h, me)
        for d in range(SPAN):
            r = (d * 2 + h) * 8
            w_ref[r : r + 8, :] = spread(base & (off == d))
            src = lax.rem(me - d + NCTX, NCTX)
            slots = slot_row(h, src)
            hit = ((slots >> 3) == me) & ((slots & 7) == sub8) & kept(h, src)
            r_ref[r : r + 8, :] = spread(hit)

    for d in range(SPAN):
        for h in range(2):
            kt = jnp.zeros((16, 128), F32)
            vt = jnp.zeros((16, 128), F32)
            for p in range(8):
                r = (d * 2 + h) * 8 + p
                w = w_ref[r : r + 1, :]
                kt += w * k_ref[p * 16 : (p + 1) * 16, h * 128 : (h + 1) * 128].astype(F32)
                vt += w * v_ref[p * 16 : (p + 1) * 16, h * 128 : (h + 1) * 128].astype(F32)
            tsend[d, h, 0:16, :] = kt.astype(BF16)
            tsend[d, h, 16:32, :] = vt.astype(BF16)
    pages = [None]
    for d in range(1, SPAN):
        pages.append(remote(tsend.at[d], trecv.at[d], pg_s.at[d], pg_r.at[d], ctxoff(d)))
        pages[d].start()

    for c in sib_q:
        c.wait_recv()
    run_m[...] = jnp.full_like(run_m, -1e30)
    run_l[...] = jnp.zeros_like(run_l)

    def split(n, carry):
        hc = n // 8
        g = lax.rem(n, 8)
        x = qb[hc, g].astype(F32) * SCALE2
        hi = x.astype(BF16)
        q2[pl.ds(pl.multiple_of(n * 128, 128), 128), 0:128] = hi
        q2[pl.ds(pl.multiple_of(n * 128, 128), 128), 128:256] = (x - hi.astype(F32)).astype(BF16)
        return carry

    lax.fori_loop(0, 16, split, 0)

    def fold(zz, masked):
        block = kvb.at[0, zz][...].reshape(SLAB, 128)
        keys = jnp.concatenate([block, block], axis=1)

        def logits(n):
            return qk(q2[n * 512 : (n + 1) * 512, :], keys)

        def absorb(n, s):
            r = slice(n * 512, (n + 1) * 512)
            parts = [s[:, t * 128 : (t + 1) * 128] for t in range(LANES)]
            if masked:
                owner = lax.rem(a + 1 - n // 2 + 2, 2)
                row = lax.broadcasted_iota(jnp.int32, (512, 128), 0) % 128
                lane = lax.broadcasted_iota(jnp.int32, (512, 128), 1)
                lim = row - lane + (y * 256 + owner * 128)
                parts = [jnp.where(lim >= t * 128, x, -1e30) for t, x in enumerate(parts)]
            m = run_m[r, :]
            top = functools.reduce(jnp.maximum, parts)
            mn = jnp.maximum(m, jnp.max(top, axis=1, keepdims=True))
            total = jnp.zeros((512, 128), F32)
            for t in range(LANES):
                e = jnp.exp2(parts[t] - mn)
                total = total + e
                prob[zz, r, t * 128 : (t + 1) * 128] = e.astype(BF16)
            run_l[r, :] = run_l[r, :] * jnp.exp2(m - mn) + total
            run_m[r, :] = mn
            mx[zz, r, :] = mn

        now = logits(0)
        for n in range(4):
            later = logits(n + 1) if n < 3 else None
            absorb(n, now)
            now = later

    def hop(i, p):
        p = jnp.int32(p)
        ring_b(i, p, 1).wait_recv()

        @pl.when(p < 4)
        def _():
            ring_b(i, p + 1, 1).start()
            ring_b(i, p, -1).wait_recv()

        @pl.when(p < 3)
        def _():
            ring_b(i, p + 1, -1).start()

        for d in range(1, NY):
            y_b(i, p, 1, d).start()

        @pl.when(p < 4)
        def _():
            for d in range(1, NY):
                y_b(i, p, -1, d).start()

        for e in range(NY):
            ring_a(i, p, 1, e).wait_recv()

            @pl.when(p < 4)
            def _():
                ring_a(i, p + 1, 1, e).start()
                ring_a(i, p, -1, e).wait_recv()

            @pl.when(p < 3)
            def _():
                ring_a(i, p + 1, -1, e).start()

    def landed(i, p):
        for d in range(1, NY):
            y_b(i, p, 1, d).wait_recv()

        @pl.when((p >= 1) & (p < 4))
        def _():
            for d in range(1, NY):
                y_b(i, p, -1, d).wait_recv()

    def both_sides(p, work):
        def side(j, c):
            up = j == 0
            zz = jnp.where(up, z - p, z + p - NZ)

            @pl.when((p >= 1) & (zz >= 0) & (up | (p < 4)))
            def _():
                work(zz)

            return c

        lax.fori_loop(0, 2, side, 0)

    def phase(p, carry):
        @pl.when(p <= 4)
        def _():
            hop(0, p)

        @pl.when(p == 1)
        def _():
            for c in ya[3:]:
                c.start()

        @pl.when(p == 2)
        def _():
            begin_own(1)
            begin_b(1)
            begin_a(1)

        pp = p - 1
        landed(0, pp)

        if True:
            @pl.when(pp == 0)
            def _():
                fold(z, True)

            both_sides(pp, lambda zz: fold(zz, False))

        @pl.when((p >= 3) & (p <= 4))
        def _():
            hop(1, p - 2)

        return carry

    lax.fori_loop(1, 6, phase, 0)

    run_m[...] = run_m[...] + jnp.log2(jnp.sum(run_l[...], axis=1, keepdims=True))
    csum[...] = jnp.zeros_like(csum)

    def colpass(zz, carry):
        def rows(i, c):
            c = list(c)
            for u in range(32):
                r = pl.ds(pl.multiple_of(i * 512 + u * 16, 16), 16)
                w = jnp.exp2(mx[zz, r, :] - run_m[r, :])
                mx[zz, r, :] = w
                for t in range(LANES):
                    x = prob[zz, r, t * 128 : (t + 1) * 128].astype(F32) * w
                    c[t] = c[t] + x[0:8] + x[8:16]
            return tuple(c)

        c = lax.fori_loop(
            0, ROWS // 512, rows, tuple(jnp.zeros((8, 128), F32) for _ in range(LANES))
        )
        for t in range(LANES):
            csum[zz, t : t + 1, :] = jnp.sum(c[t], axis=0, keepdims=True)
        return carry

    def c1(d):
        zz = lax.rem(z - d + NZ, NZ)
        return remote(csum.at[zz], csr.at[d], c1_s.at[d], c1_r.at[d], zoff(-d))

    def columns(k, carry):
        step = (k + 1) // 2
        d = jnp.where(lax.rem(k, 2) == 1, 4 - step, 4 + step)

        @pl.when(k == 4)
        def _():
            hop(1, 3)

        @pl.when((k == 7) | (d <= z))
        def _():
            colpass(jnp.where(k == 7, z, z - d), 0)

        @pl.when(k < 7)
        def _():
            c1(d).start()

        return carry

    lax.fori_loop(0, 8, columns, 0)

    acc[...] = jnp.zeros_like(acc)
    lane = lax.broadcasted_iota(jnp.int32, (8, 128), 1)
    sub = lax.broadcasted_iota(jnp.int32, (8, 128), 0)

    def weigh(zz):
        vals = kvb.at[1, zz][...].reshape(SLAB, 128)
        acc[...] += mx[zz] * jnp.dot(prob[zz], vals, preferred_element_type=F32)

    def weigh_phases(first, last):
        def one(p, c):
            landed(1, p)

            @pl.when(p == 0)
            def _():
                weigh(z)

            both_sides(p, weigh)
            return c

        lax.fori_loop(first, last, one, 0)

    weigh_phases(0, 2)
    hop(1, 4)

    total = csum[z]
    for d in range(1, NZ):
        c1(d).wait_recv()
        total = total + csr[d]
    for t in range(8):
        tot8[t] = jnp.broadcast_to(total[t : t + 1, :], (8, 128))
    c2 = [None]
    for d in range(1, 8):
        c2.append(
            remote(tot8.at[lax.rem(me8 + d, 8)], t2.at[d], c2_s.at[d], c2_r.at[d], slaboff(d))
        )
        c2[d].start()

    weigh_phases(2, 4)

    same = tot8[me8]
    other = jnp.zeros((8, 128), F32)
    for d in range(1, 8):
        c2[d].wait_recv()
        if d % 2 == 0:
            same = same + t2[d]
        else:
            other = other + t2[d]
    pos = me * BLK + lane
    factor = (NCTX * BLK / 8.0) / (NCTX * BLK - pos).astype(F32)
    col = [jnp.where(a == 0, same, other) * factor, jnp.where(a == 0, other, same) * factor]
    impb[...] = col[0] + col[1]
    im = [None]
    for d in range(1, NX):
        im.append(
            remote(impb, impr.at[d], im_s.at[d], im_r.at[d], (me, lax.rem(hx + d, NX)))
        )
        im[d].start()
    means = [
        jnp.sum(jnp.where(lane // 16 == sub, c, 0.0), axis=1, keepdims=True) / 16.0 for c in col
    ]
    for d in range(SPAN):
        for h in range(2):
            r = (d * 2 + h) * 8
            ssend[d, h : h + 1, :] = jnp.sum(w_ref[r : r + 8, :] * means[h], axis=0, keepdims=True)
    sc = [None]
    for d in range(1, SPAN):
        sc.append(remote(ssend.at[d], srecv.at[d], sc_s.at[d], sc_r.at[d], ctxoff(d)))
        sc[d].start()

    for d in range(1, SPAN):
        pages[d].wait_recv()
    for h in range(2):
        got = [
            (tsend if d == 0 else trecv)[d, h].astype(F32) for d in range(SPAN)
        ]
        place = [r_ref[(d * 2 + h) * 8 : (d * 2 + h) * 8 + 8, :] for d in range(SPAN)]
        scales = []
        for n in range(2):
            rows = [
                functools.reduce(
                    jnp.add, [place[d] * got[d][t : t + 1, :] for d in range(SPAN)]
                )
                for t in range(n * 16, n * 16 + 16)
            ]
            big = functools.reduce(jnp.maximum, [jnp.abs(x) for x in rows])
            amax = jnp.max(big, axis=1, keepdims=True)
            scales.append(amax / 7.0)
            for t, x in enumerate(rows):
                c = (n * 16 + t) * 128
                tile_ref[0, h, :, c : c + 128] = (x * 7.0 / (amax + 1e-6)).astype(BF16)
            if n == 0:
                low = functools.reduce(jnp.minimum, rows)
                high = functools.reduce(jnp.maximum, rows)
                for slot in range(8):
                    bound_ref[0, h, slot, 0:1, :] = low[slot : slot + 1, :]
                    bound_ref[0, h, slot, 1:2, :] = high[slot : slot + 1, :]
        for n in range(2):
            row = jnp.sum(jnp.where(lane == sub, scales[n], 0.0), axis=0, keepdims=True)
            scale_ref[0, h, n : n + 1, :] = row[:, 0:8]

    weigh_phases(4, 5)
    outs = []
    for g in range(8):
        osend[g] = acc[g * 128 : (g + 1) * 128, :].astype(BF16)
        outs.append(
            remote(osend.at[g], att_ref.at[:, cols(a * 8 + g)], o_s.at[g], o_r.at[g], sib)
        )
        outs[g].start()
    for g in range(8):
        att_ref[:, cols(a * 8 + g)] = acc[1024 + g * 128 : 1152 + g * 128, :].astype(BF16)

    for d in range(1, SPAN):
        sc[d].wait_recv()
    for h in range(2):
        got = jnp.zeros((8, 128), F32)
        for d in range(SPAN):
            r = (d * 2 + h) * 8
            src = ssend if d == 0 else srecv
            got += r_ref[r : r + 8, :] * src[d, h : h + 1, :]
        row = jnp.sum(jnp.where(lane == sub, got, 0.0), axis=0, keepdims=True)
        score_ref[0, h : h + 1, :] = row[:, 0:8]
    imp = impb[...]
    for d in range(1, NX):
        im[d].wait_recv()
        imp = imp + impr[d]
    imp_ref[...] = imp[0:1, :]

    for g in range(8):
        outs[g].wait()
    for c in sib_kv + ya + sib_q:
        c.wait_send()
    for i in range(2):
        for d in range(1, NY):
            y_b(i, 0, 1, d).wait_send()
        for p in range(1, 5):
            signs = (1, -1) if p < 4 else (1,)
            for s in signs:
                for e in range(NY):
                    ring_a(i, p, s, e).wait_send()
                ring_b(i, p, s).wait_send()
                for d in range(1, NY):
                    y_b(i, p, s, d).wait_send()
    for d in range(1, NZ):
        c1(d).wait_send()
    for group in (pages, c2, im, sc):
        for c in group[1:]:
            c.wait_send()


def hand_over_kernel(*refs):
    for i in range(6):
        refs[6 + i][...] = refs[i][...]


def on_device(queries, key_states, value_states, keep_pages, keep_count, dest_slot):
    vmem = pl.BlockSpec(memory_space=pltpu.VMEM)
    dma = pltpu.SemaphoreType.DMA
    call = pl.pallas_call(
        main_kernel,
        out_shape=[
            jax.ShapeDtypeStruct((BLK, 2048), BF16),
            jax.ShapeDtypeStruct((1, 128), F32),
            jax.ShapeDtypeStruct((1, 2, 8, 4096), BF16),
            jax.ShapeDtypeStruct((1, 2, 2, 8), F32),
            jax.ShapeDtypeStruct((1, 2, 8, 2, 128), F32),
            jax.ShapeDtypeStruct((1, 2, 8), F32),
        ],
        in_specs=[vmem] * 6,
        out_specs=[vmem] * 6,
        scratch_shapes=[
            pltpu.VMEM((128, 128), F32),
            pltpu.VMEM((128, 128), F32),
            pltpu.VMEM((2, 8, BLK, 128), BF16),
            pltpu.VMEM((ROWS, 256), BF16),
            pltpu.VMEM((2, NZ, NY, NC, BLK, 128), BF16),
            pltpu.VMEM((NZ, ROWS, SLAB), BF16),
            pltpu.VMEM((NZ, ROWS, 128), F32),
            pltpu.VMEM((ROWS, 128), F32),
            pltpu.VMEM((ROWS, 128), F32),
            pltpu.VMEM((ROWS, 128), F32),
            pltpu.VMEM((8, BLK, 128), BF16),
            pltpu.VMEM((NZ, 8, 128), F32),
            pltpu.VMEM((NZ, 8, 128), F32),
            pltpu.VMEM((8, 8, 128), F32),
            pltpu.VMEM((8, 8, 128), F32),
            pltpu.VMEM((8, 128), F32),
            pltpu.VMEM((NX, 8, 128), F32),
            pltpu.VMEM((SPAN, 2, 32, 128), BF16),
            pltpu.VMEM((SPAN, 2, 32, 128), BF16),
            pltpu.VMEM((SPAN, 8, 128), F32),
            pltpu.VMEM((SPAN, 8, 128), F32),
            dma((10,)),
            dma((10,)), dma((10,)),
            dma((2, NY)), dma((2, NY)),
            dma((2, 2, 5, NY)), dma((2, 2, 5, NY)),
            dma((2, 2, 5, NY)), dma((2, 2, 5, NY)),
            dma((2, 2, 5)), dma((2, 2, 5)),
            dma((SPAN,)), dma((SPAN,)),
            dma((NZ,)), dma((NZ,)),
            dma((8,)), dma((8,)),
            dma((NX,)), dma((NX,)),
            dma((SPAN,)), dma((SPAN,)),
            dma((8,)), dma((8,)),
        ],
        compiler_params=pltpu.CompilerParams(
            collective_id=0, has_side_effects=True, vmem_limit_bytes=62 * 2**20
        ),
    )
    slots = jnp.transpose(dest_slot, (0, 2, 1))
    made = call(queries, key_states, value_states, keep_pages, keep_count, slots)
    hand_over = pl.pallas_call(
        hand_over_kernel,
        out_shape=[jax.ShapeDtypeStruct(x.shape, x.dtype) for x in made],
        in_specs=[vmem] * 6,
        out_specs=[vmem] * 6,
    )
    att, imp, tiles, scale, bound, score = hand_over(*made)
    return (att, imp[0], tiles, jnp.transpose(scale, (0, 1, 3, 2)), bound, score)


def solution(mesh):
    in_specs = (
        P("ctx", "head"),
        P("ctx", "head"),
        P("ctx", "head"),
        P("head", "ctx", None),
        P("head", None),
        P("head", None, None),
    )
    out_specs = (
        P("ctx", "head"),
        P("ctx"),
        P("ctx", "head", None, None),
        P("ctx", "head", None, None),
        P("ctx", "head", None, None, None),
        P("ctx", "head", None),
    )
    return jax.shard_map(
        on_device, mesh=mesh, in_specs=in_specs, out_specs=out_specs, check_vma=False
    )
```

```python
import functools

import jax
import jax.numpy as jnp
from jax import lax
from jax.experimental import pallas as pl
from jax.experimental.pallas import tpu as pltpu
from jax.sharding import PartitionSpec as P

MESH = pl.DeviceIdType.MESH
F32 = jnp.float32
BF16 = jnp.bfloat16
NZ, NY, NC, NX = 8, 4, 2, 4
NCTX = NZ * NY * NC
BLK = 128
SLAB = NY * NC * BLK
ROWS = 2 * 8 * BLK
SPAN = 8
SCALE2 = 1.4426950408889634 / 128.0**0.5
LANES = SLAB // 128


def qk(a, b):
    return lax.dot_general(a, b, (((1,), (1,)), ((), ())), preferred_element_type=F32)


def main_kernel(
    q_ref, k_ref, v_ref, pages_ref, count_ref, slot_ref,
    att_ref, imp_ref, tile_ref, scale_ref, bound_ref, score_ref,
    w_ref, r_ref, qb, q2, kvb, prob, mx, run_m, run_l, acc, osend, csum, csr, tot8, t2, impb, impr, tsend, trecv,
    ssend, srecv, loc_sem, sib_s, sib_r, ya_s, ya_r, yb_s, yb_r, ra_s, ra_r, rb_s, rb_r,
    pg_s, pg_r, c1_s, c1_r, c2_s, c2_r, im_s, im_r, sc_s, sc_r, o_s, o_r,
):
    me = lax.axis_index("ctx")
    hx = lax.axis_index("head")
    z = me // 8
    y = lax.rem(me // 2, 4)
    a = lax.rem(me, 2)
    b = 1 - a
    me8 = lax.rem(me, 8)

    def at(zz, yy, cc):
        return (zz * 8 + yy * 2 + cc, hx)

    def zoff(d):
        return at(lax.rem(z + d + NZ, NZ), y, a)

    def yoff(d):
        return at(z, lax.rem(y + d, NY), a)

    def slaboff(d):
        return (z * 8 + lax.rem(me8 + d, 8), hx)

    def ctxoff(d):
        return (lax.rem(me + d + NCTX, NCTX), hx)

    sib = at(z, y, b)

    def remote(src, dst, ss, rs, dev):
        return pltpu.make_async_remote_copy(
            src_ref=src, dst_ref=dst, send_sem=ss, recv_sem=rs, device_id=dev, device_id_type=MESH
        )

    bar = pltpu.get_barrier_semaphore()
    peers = [zoff(d) for d in range(1, 8)] + [slaboff(d) for d in range(1, 8)]
    peers += [(me, lax.rem(hx + d, NX)) for d in range(1, NX)]
    peers += [ctxoff(d) for d in range(1, SPAN)] + [ctxoff(-d) for d in range(1, SPAN)]
    for dev in peers:
        pl.semaphore_signal(bar, inc=1, device_id=dev, device_id_type=MESH)
    pl.semaphore_wait(bar, len(peers))

    kv_in = (k_ref, v_ref)

    def cols(g):
        return pl.ds(pl.multiple_of(g * 128, 128), 128)

    local = []
    sib_kv = []
    ya = []
    for i in range(2):
        own = kv_in[i].at[:, cols(a)]
        local.append(pltpu.make_async_copy(own, kvb.at[i, z, y, a], loc_sem.at[i]))
        sib_kv.append(
            remote(kv_in[i].at[:, cols(b)], kvb.at[i, z, y, a], sib_s.at[i], sib_r.at[i], sib)
        )
        for d in range(1, NY):
            ya.append(
                remote(own, kvb.at[i, z, y, a], ya_s.at[i, d], ya_r.at[i, d], yoff(d))
            )
    sib_q = []
    for g in range(8):
        local.append(
            pltpu.make_async_copy(q_ref.at[:, cols(a * 8 + g)], qb.at[1, g], loc_sem.at[2 + g])
        )
        sib_q.append(
            remote(q_ref.at[:, cols(b * 8 + g)], qb.at[0, g], sib_s.at[2 + g], sib_r.at[2 + g], sib)
        )
    for c in [sib_kv[0]] + local + ya[:3] + sib_q + [sib_kv[1]]:
        c.start()

    def ring_a(i, p, sign, e):
        zz = lax.rem(z - sign * (p - 1) + 2 * NZ, NZ)
        blk = kvb.at[i, zz, lax.rem(y + e, NY), a]
        k = 0 if sign > 0 else 1
        return remote(blk, blk, ra_s.at[i, k, p, e], ra_r.at[i, k, p, e], zoff(sign))

    def ring_b(i, p, sign):
        zz = lax.rem(z - sign * (p - 1) + 2 * NZ, NZ)
        blk = kvb.at[i, zz, y, b]
        k = 0 if sign > 0 else 1
        return remote(blk, blk, rb_s.at[i, k, p], rb_r.at[i, k, p], zoff(sign))

    def y_b(i, p, sign, d):
        zz = lax.rem(z - sign * p + 2 * NZ, NZ)
        blk = kvb.at[i, zz, y, b]
        k = 0 if sign > 0 else 1
        return remote(blk, blk, yb_s.at[i, k, p, d], yb_r.at[i, k, p, d], yoff(d))

    def begin_b(i):
        sib_kv[i].wait_recv()
        ring_b(i, 1, 1).start()
        ring_b(i, 1, -1).start()
        for d in range(1, NY):
            y_b(i, 0, 1, d).start()

    def begin_own(i):
        local[i].wait()
        ring_a(i, 1, 1, 0).start()
        ring_a(i, 1, -1, 0).start()

    def begin_a(i):
        for d in range(1, NY):
            ya[i * 3 + NY - d - 1].wait_recv()
            ring_a(i, 1, 1, d).start()
            ring_a(i, 1, -1, d).start()

    begin_own(0)
    begin_b(0)
    for c in local[2:]:
        c.wait()
    begin_a(0)
    for c in ya[3:]:
        c.start()

    sub8 = lax.broadcasted_iota(jnp.int32, (8, 8), 0)
    lane8 = lax.broadcasted_iota(jnp.int32, (8, 8), 1)
    lane64 = lax.broadcasted_iota(jnp.int32, (1, 64), 1)
    lane864 = lax.broadcasted_iota(jnp.int32, (8, 64), 1)

    def kept(h, src):
        row = jnp.where(lane64 == src, count_ref[h : h + 1, :].astype(F32), 0.0)
        return lane8.astype(F32) < jnp.sum(row, axis=1, keepdims=True)

    def spread(hit):
        return jnp.broadcast_to(
            jnp.sum(jnp.where(hit, 1.0, 0.0), axis=1, keepdims=True), (8, 128)
        )

    def slot_row(h, src):
        col = jnp.sum(
            jnp.where(lane864 == src, slot_ref[h].astype(F32), 0.0), axis=1, keepdims=True
        )
        row = jnp.sum(jnp.where(sub8 == lane8, col, 0.0), axis=0, keepdims=True)
        return row.astype(jnp.int32)

    for h in range(2):
        slots = slot_row(h, me)
        off = ((slots >> 3) - me) & (NCTX - 1)
        base = (pages_ref[h, 0:1, :] == sub8) & kept(h, me)
        for d in range(SPAN):
            r = (d * 2 + h) * 8
            w_ref[r : r + 8, :] = spread(base & (off == d))
            src = lax.rem(me - d + NCTX, NCTX)
            slots = slot_row(h, src)
            hit = ((slots >> 3) == me) & ((slots & 7) == sub8) & kept(h, src)
            r_ref[r : r + 8, :] = spread(hit)

    for d in range(SPAN):
        for h in range(2):
            kt = jnp.zeros((16, 128), F32)
            vt = jnp.zeros((16, 128), F32)
            for p in range(8):
                r = (d * 2 + h) * 8 + p
                w = w_ref[r : r + 1, :]
                kt += w * k_ref[p * 16 : (p + 1) * 16, h * 128 : (h + 1) * 128].astype(F32)
                vt += w * v_ref[p * 16 : (p + 1) * 16, h * 128 : (h + 1) * 128].astype(F32)
            tsend[d, h, 0:16, :] = kt.astype(BF16)
            tsend[d, h, 16:32, :] = vt.astype(BF16)
    pages = [None]
    for d in range(1, SPAN):
        pages.append(remote(tsend.at[d], trecv.at[d], pg_s.at[d], pg_r.at[d], ctxoff(d)))
        pages[d].start()

    for c in sib_q:
        c.wait_recv()
    run_m[...] = jnp.full_like(run_m, -1e30)
    run_l[...] = jnp.zeros_like(run_l)

    def split(n, carry):
        hc = n // 8
        g = lax.rem(n, 8)
        x = qb[hc, g].astype(F32) * SCALE2
        hi = x.astype(BF16)
        q2[pl.ds(pl.multiple_of(n * 128, 128), 128), 0:128] = hi
        q2[pl.ds(pl.multiple_of(n * 128, 128), 128), 128:256] = (x - hi.astype(F32)).astype(BF16)
        return carry

    lax.fori_loop(0, 16, split, 0)

    def fold(zz, masked):
        block = kvb.at[0, zz][...].reshape(SLAB, 128)
        keys = jnp.concatenate([block, block], axis=1)

        def logits(n):
            return qk(q2[n * 512 : (n + 1) * 512, :], keys)

        def absorb(n, s):
            r = slice(n * 512, (n + 1) * 512)
            parts = [s[:, t * 128 : (t + 1) * 128] for t in range(LANES)]
            if masked:
                owner = lax.rem(a + 1 - n // 2 + 2, 2)
                row = lax.broadcasted_iota(jnp.int32, (512, 128), 0) % 128
                lane = lax.broadcasted_iota(jnp.int32, (512, 128), 1)
                lim = row - lane + (y * 256 + owner * 128)
                parts = [jnp.where(lim >= t * 128, x, -1e30) for t, x in enumerate(parts)]
            m = run_m[r, :]
            top = functools.reduce(jnp.maximum, parts)
            mn = jnp.maximum(m, jnp.max(top, axis=1, keepdims=True))
            total = jnp.zeros((512, 128), F32)
            for t in range(LANES):
                e = jnp.exp2(parts[t] - mn)
                total = total + e
                prob[zz, r, t * 128 : (t + 1) * 128] = e.astype(BF16)
            run_l[r, :] = run_l[r, :] * jnp.exp2(m - mn) + total
            run_m[r, :] = mn
            mx[zz, r, :] = mn

        now = logits(0)
        for n in range(4):
            later = logits(n + 1) if n < 3 else None
            absorb(n, now)
            now = later

    def hop(i, p):
        p = jnp.int32(p)
        ring_b(i, p, 1).wait_recv()

        @pl.when(p < 4)
        def _():
            ring_b(i, p + 1, 1).start()
            ring_b(i, p, -1).wait_recv()

        @pl.when(p < 3)
        def _():
            ring_b(i, p + 1, -1).start()

        for d in range(1, NY):
            y_b(i, p, 1, d).start()

        @pl.when(p < 4)
        def _():
            for d in range(1, NY):
                y_b(i, p, -1, d).start()

        for e in range(NY):
            ring_a(i, p, 1, e).wait_recv()

            @pl.when(p < 4)
            def _():
                ring_a(i, p + 1, 1, e).start()
                ring_a(i, p, -1, e).wait_recv()

            @pl.when(p < 3)
            def _():
                ring_a(i, p + 1, -1, e).start()

    def landed(i, p):
        for d in range(1, NY):
            y_b(i, p, 1, d).wait_recv()

        @pl.when((p >= 1) & (p < 4))
        def _():
            for d in range(1, NY):
                y_b(i, p, -1, d).wait_recv()

    def both_sides(p, work):
        def side(j, c):
            up = j == 0
            zz = jnp.where(up, z - p, z + p - NZ)

            @pl.when((p >= 1) & (zz >= 0) & (up | (p < 4)))
            def _():
                work(zz)

            return c

        lax.fori_loop(0, 2, side, 0)

    def phase(p, carry):
        @pl.when(p <= 4)
        def _():
            hop(0, p)

        @pl.when(p == 1)
        def _():
            begin_own(1)
            begin_b(1)
            begin_a(1)

        pp = p - 1
        landed(0, pp)

        if True:
            @pl.when(pp == 0)
            def _():
                fold(z, True)

            both_sides(pp, lambda zz: fold(zz, False))

        @pl.when((p >= 3) & (p <= 4))
        def _():
            hop(1, p - 2)

        return carry

    lax.fori_loop(1, 6, phase, 0)

    run_m[...] = run_m[...] + jnp.log2(jnp.sum(run_l[...], axis=1, keepdims=True))
    csum[...] = jnp.zeros_like(csum)

    def colpass(zz, carry):
        def rows(i, c):
            c = list(c)
            for u in range(32):
                r = pl.ds(pl.multiple_of(i * 512 + u * 16, 16), 16)
                w = jnp.exp2(mx[zz, r, :] - run_m[r, :])
                mx[zz, r, :] = w
                for t in range(LANES):
                    x = prob[zz, r, t * 128 : (t + 1) * 128].astype(F32) * w
                    c[t] = c[t] + x[0:8] + x[8:16]
            return tuple(c)

        c = lax.fori_loop(
            0, ROWS // 512, rows, tuple(jnp.zeros((8, 128), F32) for _ in range(LANES))
        )
        for t in range(LANES):
            csum[zz, t : t + 1, :] = jnp.sum(c[t], axis=0, keepdims=True)
        return carry

    def c1(d):
        zz = lax.rem(z - d + NZ, NZ)
        return remote(csum.at[zz], csr.at[d], c1_s.at[d], c1_r.at[d], zoff(-d))

    def columns(k, carry):
        step = (k + 1) // 2
        d = jnp.where(lax.rem(k, 2) == 1, 4 - step, 4 + step)

        @pl.when(k == 4)
        def _():
            hop(1, 3)

        @pl.when((k == 7) | (d <= z))
        def _():
            colpass(jnp.where(k == 7, z, z - d), 0)

        @pl.when(k < 7)
        def _():
            c1(d).start()

        return carry

    lax.fori_loop(0, 8, columns, 0)

    acc[...] = jnp.zeros_like(acc)
    lane = lax.broadcasted_iota(jnp.int32, (8, 128), 1)
    sub = lax.broadcasted_iota(jnp.int32, (8, 128), 0)

    def weigh(zz):
        vals = kvb.at[1, zz][...].reshape(SLAB, 128)
        acc[...] += mx[zz] * jnp.dot(prob[zz], vals, preferred_element_type=F32)

    def weigh_phases(first, last):
        def one(p, c):
            landed(1, p)

            @pl.when(p == 0)
            def _():
                weigh(z)

            both_sides(p, weigh)
            return c

        lax.fori_loop(first, last, one, 0)

    weigh_phases(0, 2)
    hop(1, 4)

    total = csum[z]
    for d in range(1, NZ):
        c1(d).wait_recv()
        total = total + csr[d]
    for t in range(8):
        tot8[t] = jnp.broadcast_to(total[t : t + 1, :], (8, 128))
    c2 = [None]
    for d in range(1, 8):
        c2.append(
            remote(tot8.at[lax.rem(me8 + d, 8)], t2.at[d], c2_s.at[d], c2_r.at[d], slaboff(d))
        )
        c2[d].start()

    weigh_phases(2, 4)

    same = tot8[me8]
    other = jnp.zeros((8, 128), F32)
    for d in range(1, 8):
        c2[d].wait_recv()
        if d % 2 == 0:
            same = same + t2[d]
        else:
            other = other + t2[d]
    pos = me * BLK + lane
    factor = (NCTX * BLK / 8.0) / (NCTX * BLK - pos).astype(F32)
    col = [jnp.where(a == 0, same, other) * factor, jnp.where(a == 0, other, same) * factor]
    impb[...] = col[0] + col[1]
    im = [None]
    for d in range(1, NX):
        im.append(
            remote(impb, impr.at[d], im_s.at[d], im_r.at[d], (me, lax.rem(hx + d, NX)))
        )
        im[d].start()
    means = [
        jnp.sum(jnp.where(lane // 16 == sub, c, 0.0), axis=1, keepdims=True) / 16.0 for c in col
    ]
    for d in range(SPAN):
        for h in range(2):
            r = (d * 2 + h) * 8
            ssend[d, h : h + 1, :] = jnp.sum(w_ref[r : r + 8, :] * means[h], axis=0, keepdims=True)
    sc = [None]
    for d in range(1, SPAN):
        sc.append(remote(ssend.at[d], srecv.at[d], sc_s.at[d], sc_r.at[d], ctxoff(d)))
        sc[d].start()

    for d in range(1, SPAN):
        pages[d].wait_recv()
    for h in range(2):
        got = [
            (tsend if d == 0 else trecv)[d, h].astype(F32) for d in range(SPAN)
        ]
        place = [r_ref[(d * 2 + h) * 8 : (d * 2 + h) * 8 + 8, :] for d in range(SPAN)]
        scales = []
        for n in range(2):
            rows = [
                functools.reduce(
                    jnp.add, [place[d] * got[d][t : t + 1, :] for d in range(SPAN)]
                )
                for t in range(n * 16, n * 16 + 16)
            ]
            big = functools.reduce(jnp.maximum, [jnp.abs(x) for x in rows])
            amax = jnp.max(big, axis=1, keepdims=True)
            scales.append(amax / 7.0)
            for t, x in enumerate(rows):
                c = (n * 16 + t) * 128
                tile_ref[0, h, :, c : c + 128] = (x * 7.0 / (amax + 1e-6)).astype(BF16)
            if n == 0:
                low = functools.reduce(jnp.minimum, rows)
                high = functools.reduce(jnp.maximum, rows)
                for slot in range(8):
                    bound_ref[0, h, slot, 0:1, :] = low[slot : slot + 1, :]
                    bound_ref[0, h, slot, 1:2, :] = high[slot : slot + 1, :]
        for n in range(2):
            row = jnp.sum(jnp.where(lane == sub, scales[n], 0.0), axis=0, keepdims=True)
            scale_ref[0, h, n : n + 1, :] = row[:, 0:8]

    weigh_phases(4, 5)
    outs = []
    for g in range(8):
        osend[g] = acc[g * 128 : (g + 1) * 128, :].astype(BF16)
        outs.append(
            remote(osend.at[g], att_ref.at[:, cols(a * 8 + g)], o_s.at[g], o_r.at[g], sib)
        )
        outs[g].start()
    for g in range(8):
        att_ref[:, cols(a * 8 + g)] = acc[1024 + g * 128 : 1152 + g * 128, :].astype(BF16)

    for d in range(1, SPAN):
        sc[d].wait_recv()
    for h in range(2):
        got = jnp.zeros((8, 128), F32)
        for d in range(SPAN):
            r = (d * 2 + h) * 8
            src = ssend if d == 0 else srecv
            got += r_ref[r : r + 8, :] * src[d, h : h + 1, :]
        row = jnp.sum(jnp.where(lane == sub, got, 0.0), axis=0, keepdims=True)
        score_ref[0, h : h + 1, :] = row[:, 0:8]
    imp = impb[...]
    for d in range(1, NX):
        im[d].wait_recv()
        imp = imp + impr[d]
    imp_ref[...] = imp[0:1, :]

    for g in range(8):
        outs[g].wait()
    for c in sib_kv + ya + sib_q:
        c.wait_send()
    for i in range(2):
        for d in range(1, NY):
            y_b(i, 0, 1, d).wait_send()
        for p in range(1, 5):
            signs = (1, -1) if p < 4 else (1,)
            for s in signs:
                for e in range(NY):
                    ring_a(i, p, s, e).wait_send()
                ring_b(i, p, s).wait_send()
                for d in range(1, NY):
                    y_b(i, p, s, d).wait_send()
    for d in range(1, NZ):
        c1(d).wait_send()
    for group in (pages, c2, im, sc):
        for c in group[1:]:
            c.wait_send()


def hand_over_kernel(*refs):
    for i in range(6):
        refs[6 + i][...] = refs[i][...]


def on_device(queries, key_states, value_states, keep_pages, keep_count, dest_slot):
    vmem = pl.BlockSpec(memory_space=pltpu.VMEM)
    dma = pltpu.SemaphoreType.DMA
    call = pl.pallas_call(
        main_kernel,
        out_shape=[
            jax.ShapeDtypeStruct((BLK, 2048), BF16),
            jax.ShapeDtypeStruct((1, 128), F32),
            jax.ShapeDtypeStruct((1, 2, 8, 4096), BF16),
            jax.ShapeDtypeStruct((1, 2, 2, 8), F32),
            jax.ShapeDtypeStruct((1, 2, 8, 2, 128), F32),
            jax.ShapeDtypeStruct((1, 2, 8), F32),
        ],
        in_specs=[vmem] * 6,
        out_specs=[vmem] * 6,
        scratch_shapes=[
            pltpu.VMEM((128, 128), F32),
            pltpu.VMEM((128, 128), F32),
            pltpu.VMEM((2, 8, BLK, 128), BF16),
            pltpu.VMEM((ROWS, 256), BF16),
            pltpu.VMEM((2, NZ, NY, NC, BLK, 128), BF16),
            pltpu.VMEM((NZ, ROWS, SLAB), BF16),
            pltpu.VMEM((NZ, ROWS, 128), F32),
            pltpu.VMEM((ROWS, 128), F32),
            pltpu.VMEM((ROWS, 128), F32),
            pltpu.VMEM((ROWS, 128), F32),
            pltpu.VMEM((8, BLK, 128), BF16),
            pltpu.VMEM((NZ, 8, 128), F32),
            pltpu.VMEM((NZ, 8, 128), F32),
            pltpu.VMEM((8, 8, 128), F32),
            pltpu.VMEM((8, 8, 128), F32),
            pltpu.VMEM((8, 128), F32),
            pltpu.VMEM((NX, 8, 128), F32),
            pltpu.VMEM((SPAN, 2, 32, 128), BF16),
            pltpu.VMEM((SPAN, 2, 32, 128), BF16),
            pltpu.VMEM((SPAN, 8, 128), F32),
            pltpu.VMEM((SPAN, 8, 128), F32),
            dma((10,)),
            dma((10,)), dma((10,)),
            dma((2, NY)), dma((2, NY)),
            dma((2, 2, 5, NY)), dma((2, 2, 5, NY)),
            dma((2, 2, 5, NY)), dma((2, 2, 5, NY)),
            dma((2, 2, 5)), dma((2, 2, 5)),
            dma((SPAN,)), dma((SPAN,)),
            dma((NZ,)), dma((NZ,)),
            dma((8,)), dma((8,)),
            dma((NX,)), dma((NX,)),
            dma((SPAN,)), dma((SPAN,)),
            dma((8,)), dma((8,)),
        ],
        compiler_params=pltpu.CompilerParams(
            collective_id=0, has_side_effects=True, vmem_limit_bytes=62 * 2**20
        ),
    )
    slots = jnp.transpose(dest_slot, (0, 2, 1))
    made = call(queries, key_states, value_states, keep_pages, keep_count, slots)
    hand_over = pl.pallas_call(
        hand_over_kernel,
        out_shape=[jax.ShapeDtypeStruct(x.shape, x.dtype) for x in made],
        in_specs=[vmem] * 6,
        out_specs=[vmem] * 6,
    )
    att, imp, tiles, scale, bound, score = hand_over(*made)
    return (att, imp[0], tiles, jnp.transpose(scale, (0, 1, 3, 2)), bound, score)


def solution(mesh):
    in_specs = (
        P("ctx", "head"),
        P("ctx", "head"),
        P("ctx", "head"),
        P("head", "ctx", None),
        P("head", None),
        P("head", None, None),
    )
    out_specs = (
        P("ctx", "head"),
        P("ctx"),
        P("ctx", "head", None, None),
        P("ctx", "head", None, None),
        P("ctx", "head", None, None, None),
        P("ctx", "head", None),
    )
    return jax.shard_map(
        on_device, mesh=mesh, in_specs=in_specs, out_specs=out_specs, check_vma=False
    )
```
